32 devices in a mesh: lat: 8 (over z, y), lon: 4 (over x, core).
Axes of the slice: x: 2, y: 2, z: 4, core: 2. Of those that a mesh axis runs over, the one named last changes fastest.
Arguments:
- fields: bfloat16 [1, 256, 256, 128], P(None, 'lat', 'lon'), may hold values from -6 to 6
- cotangent: bfloat16 [1, 256, 256, 128], P(None, 'lat', 'lon'), may hold values from -6 to 6
- spectral_weight: bfloat16 [256, 2, 128, 128], P('lat'), may hold values from -0.375 to 0.375
- local_weight: bfloat16 [3, 128, 128], replicated, may hold values from -0.3125 to 0.3125
- filter_basis: bfloat16 [3, 256, 3, 17], replicated, may hold values from -0.83984375 to 0.83984375
- neighbor_rows: int32 [256, 3], replicated, may hold values from 0 to 255, as said below
Outputs:
- block_output: bfloat16 [1, 256, 256, 128], P(None, 'lat', 'lon')
- input_grad: bfloat16 [1, 256, 256, 128], P(None, 'lat', 'lon')
The draws below stay inside these ranges and needn't reach their ends.
Inputs may be any that keep to these rules, and one draw needn't show every extreme that they name: `neighbor_rows`: row i lists the rows that feed output latitude i: its first entry is max(i - 8, 0), its last min(i + 8, 255), and every entry lies within 8 of i.
All inputs are finite; a program needn't handle non-finite values.
Results may differ from the reference program's by a relative error of at most 0.015.
Values may be sent and summed in bfloat16 or wider, within the bound.
A program may use at most 128 MiB of HBM per device.

```python
import math
import jax
import jax.numpy as jnp
from jax import lax

MEM = 1
C = 128
MDEV = 16
KB = 3
NB = 3
HW = 8
SUP = 17
NLAT = 256
NLON = 256
MM = 64
L = 256


def draw_neighbor_rows(key, part):
    row_ids = jnp.arange(NLAT, dtype=jnp.int32)[:, None]
    offsets = jax.random.randint(key, (NLAT, NB), -HW, HW + 1, dtype=jnp.int32)
    column_ids = jnp.arange(NB, dtype=jnp.int32)[None, :]
    offsets = jnp.where(column_ids == 0, -HW, jnp.where(column_ids == NB - 1, HW, offsets))
    return jnp.clip(row_ids + offsets, 0, NLAT - 1).astype(jnp.int32)


def shard_levels(own_key, dims, shards, smallest, high):
    def one(position, shards_of):
        steps = jax.random.uniform(jax.random.fold_in(jax.random.fold_in(own_key, 6), position), (shards_of,), jnp.float32, smallest / len(shards), high / len(shards))
        return jnp.repeat(jnp.exp(steps), dims[position] // shards_of).reshape((-1,) + (1,) * (len(dims) - position - 1))

    factor_of = one(*shards[0])
    for cut in shards[1:]:
        factor_of = factor_of * one(*cut)
    return factor_of


def normal_values(stream_key, shape, deviation, limit, pieces=(), kind=jnp.bfloat16):
    values = jax.random.normal(stream_key, shape, jnp.float32) * deviation
    if len(pieces) > 0:
        values = shard_levels(stream_key, shape, pieces, -0.22, 0.18) * values
    return jnp.clip(values, min=-limit, max=limit).astype(kind)


def setup_inputs(seed: int = 0) -> dict:
    keys = jax.random.split(jax.random.key(seed), 7)
    fields = normal_values(keys[0], (MEM, NLAT, NLON, C), 1.0, 6.0, ((1, 8), (2, 4)))
    cotangent = normal_values(keys[1], (MEM, NLAT, NLON, C), 1.0, 6.0, ((1, 8), (2, 4)))
    spectral_weight = normal_values(keys[2], (L, 2, C, C), (2 * C) ** -0.5, 0.375, ((0, 8),))
    local_weight = normal_values(keys[3], (KB, C, C), (KB * C) ** -0.5, 0.3125)
    filter_basis = normal_values(keys[4], (KB, NLAT, NB, SUP), 0.14, 0.83984375)
    neighbor_rows = draw_neighbor_rows(jax.random.fold_in(keys[6], 71), 0)
    return {"fields": fields, "cotangent": cotangent, "spectral_weight": spectral_weight, "local_weight": local_weight, "filter_basis": filter_basis, "neighbor_rows": neighbor_rows}


TANH_SCALE = 0.7978845608028654
CUBIC_TERM = 0.044715

def rounded(values):
    return lax.optimization_barrier(values.astype(jnp.bfloat16))

def gelu_parts(values):
    tanh_input = TANH_SCALE * (values + CUBIC_TERM * values * values * values)
    hyper = jnp.tanh(tanh_input)
    result = 0.5 * values * (1.0 + hyper)
    derivative = 0.5 * (1.0 + hyper) + 0.5 * values * (1.0 - hyper * hyper) * TANH_SCALE * (1.0 + 3.0 * CUBIC_TERM * values * values)
    return (result, derivative)

def mode_tables(lon_count, mode_count):
    angles_int = jnp.arange(lon_count, dtype=jnp.int32)[:, None] * jnp.arange(mode_count, dtype=jnp.int32)[None, :] % lon_count
    angles = angles_int.astype(jnp.float32) * (2.0 * math.pi / lon_count)
    stacked = jnp.stack([jnp.cos(angles), -jnp.sin(angles)], axis=1)
    orders = jnp.arange(mode_count, dtype=jnp.int32)
    factor = jnp.where(orders == 0, 1.0, 2.0).astype(jnp.float32)
    to_modes = (stacked * (2.0 * math.pi / lon_count)).astype(jnp.bfloat16)
    from_modes = (stacked * factor[None, None, :]).astype(jnp.bfloat16)
    return (to_modes, from_modes)

def combine_steps(earlier, later):
    early_aa, early_ab, early_ba, early_bb, early_log = earlier
    late_aa, late_ab, late_ba, late_bb, late_log = later
    joint_aa = late_aa * early_aa + late_ab * early_ba
    joint_ab = late_aa * early_ab + late_ab * early_bb
    joint_ba = late_ba * early_aa + late_bb * early_ba
    joint_bb = late_ba * early_ab + late_bb * early_bb
    largest = jnp.maximum(jnp.maximum(jnp.abs(joint_aa), jnp.abs(joint_ab)), jnp.maximum(jnp.abs(joint_ba), jnp.abs(joint_bb)))
    return (joint_aa / largest, joint_ab / largest, joint_ba / largest, joint_bb / largest, early_log + late_log + jnp.log(largest))

def legendre_rows(orders, degree_count, lat_count):
    colatitude = math.pi * (jnp.arange(lat_count, dtype=jnp.float32) + 0.5) / lat_count
    cosine = jnp.cos(colatitude)
    sine_part = jnp.sin(colatitude)
    order_real = orders.astype(jnp.float32)
    seed_log = 0.5 * (jnp.log((2.0 * order_real + 1.0) / (4.0 * math.pi)) + lax.lgamma(order_real + 0.5) - lax.lgamma(order_real + 1.0) - 0.5 * math.log(math.pi))
    seed_log = seed_log[:, None] + order_real[:, None] * jnp.log(sine_part)[None, :]
    degree_ints = jnp.arange(degree_count, dtype=jnp.int32)
    degree_real = degree_ints.astype(jnp.float32)[:, None]
    order_row = order_real[None, :]
    active = degree_ints[:, None] > orders[None, :]
    forward_gain = jnp.sqrt(jnp.maximum(4.0 * degree_real * degree_real - 1.0, 1.0) / jnp.maximum(degree_real * degree_real - order_row * order_row, 1.0))
    backward_gain = jnp.sqrt(jnp.maximum((degree_real - 1.0) ** 2 - order_row * order_row, 0.0) / jnp.maximum(4.0 * (degree_real - 1.0) ** 2 - 1.0, 1.0))
    grid_shape = (degree_count, orders.shape[0], lat_count)
    active_full = jnp.broadcast_to(active[:, :, None], grid_shape)
    entry_aa = jnp.where(active_full, forward_gain[:, :, None] * cosine[None, None, :], 1.0)
    entry_ab = jnp.where(active_full, jnp.broadcast_to(-(forward_gain * backward_gain)[:, :, None], grid_shape), 0.0)
    entry_ba = jnp.where(active_full, 1.0, 0.0).astype(jnp.float32)
    entry_bb = jnp.where(active_full, 0.0, 1.0).astype(jnp.float32)
    log_start = jnp.zeros(grid_shape, jnp.float32)
    prefix = lax.associative_scan(combine_steps, (entry_aa, entry_ab, entry_ba, entry_bb, log_start), axis=0)
    values = prefix[0] * jnp.exp(prefix[4] + seed_log[None, :, :])
    kept = degree_ints[:, None, None] >= orders[None, :, None]
    return jnp.where(kept, values, 0.0).transpose(1, 0, 2)

def degree_pass(data, use_weights, to_degrees):
    mem_count = data.shape[0]
    count_in = data.shape[1]
    block_count = MM // MDEV
    blocks = data.reshape(mem_count, count_in, 2, block_count, MDEV, C).transpose(3, 0, 1, 2, 4, 5)
    colatitude = math.pi * (jnp.arange(NLAT, dtype=jnp.float32) + 0.5) / NLAT
    quadrature = math.pi / NLAT * jnp.sin(colatitude)

    def one_block(packed):
        block_id, block_data = packed
        orders = block_id * MDEV + jnp.arange(MDEV, dtype=jnp.int32)
        degree_table = legendre_rows(orders, L, NLAT)
        if use_weights:
            degree_table = degree_table * quadrature[None, None, :]
        degree_table = rounded(degree_table).astype(jnp.float32)
        if to_degrees:
            return rounded(jnp.einsum('aikmc,mli->alkmc', block_data.astype(jnp.float32), degree_table))
        return rounded(jnp.einsum('alkmc,mli->aikmc', block_data.astype(jnp.float32), degree_table))
    result = lax.map(one_block, (jnp.arange(block_count, dtype=jnp.int32), blocks))
    count_out = result.shape[2]
    return result.transpose(1, 2, 3, 0, 4, 5).reshape(mem_count, count_out, 2, MM, C)

def local_forward(fields, filter_basis, neighbor_rows, local_weight):
    weight_real = local_weight.astype(jnp.float32)

    def one_row(row_id):
        sources = jnp.take(fields, neighbor_rows[row_id], axis=1).astype(jnp.float32)
        basis_row = lax.dynamic_index_in_dim(filter_basis, row_id, axis=1, keepdims=False).astype(jnp.float32)
        running = jnp.zeros((KB, sources.shape[0], NLON, C), jnp.float32)
        for offset in range(SUP):
            rolled = jnp.roll(sources, HW - offset, axis=2)
            running = running + jnp.einsum('kb,abfc->kafc', basis_row[:, :, offset], rolled)
        local_terms = rounded(running).astype(jnp.float32)
        return jnp.einsum('kafc,kcd->afd', local_terms, weight_real)
    result = lax.map(one_row, jnp.arange(NLAT, dtype=jnp.int32))
    return result.transpose(1, 0, 2, 3)

def local_backward(grad_mix, filter_basis, neighbor_rows, local_weight):
    weight_real = local_weight.astype(jnp.float32)
    mem_count = grad_mix.shape[0]

    def one_row(running, row_id):
        grad_row = lax.dynamic_index_in_dim(grad_mix, row_id, axis=1, keepdims=False).astype(jnp.float32)
        local_row = rounded(jnp.einsum('afd,kcd->kafc', grad_row, weight_real)).astype(jnp.float32)
        basis_row = lax.dynamic_index_in_dim(filter_basis, row_id, axis=1, keepdims=False).astype(jnp.float32)
        contrib = jnp.zeros((NB, mem_count, NLON, C), jnp.float32)
        for offset in range(SUP):
            rolled = jnp.roll(local_row, offset - HW, axis=2)
            contrib = contrib + jnp.einsum('kb,kafc->bafc', basis_row[:, :, offset], rolled)
        running = running.at[:, neighbor_rows[row_id]].add(contrib.transpose(1, 0, 2, 3))
        return (running, None)
    start_sum = jnp.zeros((mem_count, NLAT, NLON, C), jnp.float32)
    running, _ = lax.scan(one_row, start_sum, jnp.arange(NLAT, dtype=jnp.int32))
    return running

def reference(fields, cotangent, spectral_weight, local_weight, filter_basis, neighbor_rows):
    to_modes, from_modes = mode_tables(NLON, MM)
    to_real = lax.optimization_barrier(to_modes).astype(jnp.float32)
    from_real = lax.optimization_barrier(from_modes).astype(jnp.float32)
    real_part = spectral_weight[:, 0]
    imag_part = spectral_weight[:, 1]
    complex_mix = jnp.stack([jnp.stack([real_part, imag_part], axis=2), jnp.stack([-imag_part, real_part], axis=2)], axis=1).astype(jnp.float32)
    fourier = rounded(jnp.einsum('aifc,fkm->aikmc', fields.astype(jnp.float32), to_real))
    harmonics = degree_pass(fourier, True, True)
    filtered = rounded(jnp.einsum('alkmc,lkcjx->aljmx', harmonics.astype(jnp.float32), complex_mix))
    zonal_modes = degree_pass(filtered, False, False)
    spectral = rounded(jnp.einsum('aikmc,fkm->aifc', zonal_modes.astype(jnp.float32), from_real))
    pre_act = spectral.astype(jnp.float32) + local_forward(fields, filter_basis, neighbor_rows, local_weight)
    activation, derivative = gelu_parts(pre_act)
    block_output = (fields.astype(jnp.float32) + activation).astype(jnp.bfloat16)
    grad_mix = rounded(cotangent.astype(jnp.float32) * derivative)
    grad_zonal = rounded(jnp.einsum('aifc,fkm->aikmc', grad_mix.astype(jnp.float32), from_real))
    grad_filtered = degree_pass(grad_zonal, False, True)
    grad_harmonics = rounded(jnp.einsum('aljmx,lkcjx->alkmc', grad_filtered.astype(jnp.float32), complex_mix))
    grad_fourier = degree_pass(grad_harmonics, True, False)
    grad_spectral = rounded(jnp.einsum('aikmc,fkm->aifc', grad_fourier.astype(jnp.float32), to_real))
    grad_sum = local_backward(grad_mix, filter_basis, neighbor_rows, local_weight)
    input_grad = (cotangent.astype(jnp.float32) + grad_spectral.astype(jnp.float32) + grad_sum).astype(jnp.bfloat16)
    return (block_output, input_grad)
```

```python
import math

import jax
import jax.numpy as jnp
from jax import lax
from jax.experimental import pallas as pl
from jax.experimental.pallas import tpu as pltpu
from jax.sharding import PartitionSpec as P

MDEV = 16
HW = 8


TANH_SCALE = 0.7978845608028654
CUBIC_TERM = 0.044715


def extended(cells, sides, width):
    for axis, dim in sides:
        count = lax.axis_size(axis)
        head = lax.slice_in_dim(cells, 0, width, axis=dim)
        tail = lax.slice_in_dim(cells, cells.shape[dim] - width, cells.shape[dim], axis=dim)
        cells = jnp.concatenate(
            [
                lax.ppermute(tail, axis, [(i, (i + 1) % count) for i in range(count)]),
                cells,
                lax.ppermute(head, axis, [((i + 1) % count, i) for i in range(count)]),
            ],
            axis=dim,
        )
    return cells


def gelu_parts(values):
    tanh_input = TANH_SCALE * (values + CUBIC_TERM * values * values * values)
    hyper = jnp.tanh(tanh_input)
    result = 0.5 * values * (1.0 + hyper)
    derivative = 0.5 * (1.0 + hyper) + 0.5 * values * (1.0 - hyper * hyper) * TANH_SCALE * (
        1.0 + 3.0 * CUBIC_TERM * values * values
    )
    return (result, derivative)


def mode_tables(lon_count, mode_count):
    angles_int = (
        jnp.arange(lon_count, dtype=jnp.int32)[:, None]
        * jnp.arange(mode_count, dtype=jnp.int32)[None, :]
        % lon_count
    )
    angles = angles_int.astype(jnp.float32) * (2.0 * math.pi / lon_count)
    stacked = jnp.stack([jnp.cos(angles), -jnp.sin(angles)], axis=1)
    orders = jnp.arange(mode_count, dtype=jnp.int32)
    factor = jnp.where(orders == 0, 1.0, 2.0).astype(jnp.float32)
    to_modes = (stacked * (2.0 * math.pi / lon_count)).astype(jnp.bfloat16)
    from_modes = (stacked * factor[None, None, :]).astype(jnp.bfloat16)
    return (to_modes, from_modes)


STEP = 16


def legendre_kernel(gain_ref, back_ref, orders_ref, trig_ref, weighted_ref, plain_ref):
    order_share, degree_count, _ = plain_ref.shape
    cosine = trig_ref[0:1, :]
    quadrature = trig_ref[1:2, :]

    def block(index, state):
        carried = []
        for e in range(order_share):
            value, previous, log_scale = state[3 * e : 3 * e + 3]
            order = orders_ref[e]
            rows = []
            for step in range(STEP):
                degree = index * STEP + step
                active = degree > order
                following = gain_ref[e, degree] * (cosine * value) - back_ref[e, degree] * previous
                previous = jnp.where(active, value, previous)
                value = jnp.where(active, following, value)
                rows.append(jnp.where(degree >= order, value, 0.0))
            stacked = jnp.concatenate(rows, axis=0) * jnp.exp(log_scale)
            place = pl.ds(pl.multiple_of(index * STEP, STEP), STEP)
            plain_ref[e, place, :] = stacked.astype(jnp.bfloat16)
            weighted_ref[e, place, :] = (stacked * quadrature).astype(jnp.bfloat16)
            largest = jnp.maximum(jnp.abs(value), jnp.abs(previous))
            carried += [value / largest, previous / largest, log_scale + jnp.log(largest)]
        return tuple(carried)

    start = []
    for e in range(order_share):
        seed = trig_ref[2 + e : 3 + e, :]
        start += [jnp.ones_like(seed), jnp.zeros_like(seed), seed]
    lax.fori_loop(0, degree_count // STEP, block, tuple(start))


def legendre_tables(orders, degree_count, lat_count):
    order_share = orders.shape[0]
    colatitude = math.pi * (jnp.arange(lat_count, dtype=jnp.float32) + 0.5) / lat_count
    sine_part = jnp.sin(colatitude)
    order_real = orders.astype(jnp.float32)
    seed_log = 0.5 * (
        jnp.log((2.0 * order_real + 1.0) / (4.0 * math.pi))
        + lax.lgamma(order_real + 0.5)
        - lax.lgamma(order_real + 1.0)
        - 0.5 * math.log(math.pi)
    )
    seed_log = seed_log[:, None] + order_real[:, None] * jnp.log(sine_part)[None, :]
    degree_real = jnp.arange(degree_count, dtype=jnp.float32)[None, :]
    order_row = order_real[:, None]
    forward_gain = jnp.sqrt(
        jnp.maximum(4.0 * degree_real * degree_real - 1.0, 1.0)
        / jnp.maximum(degree_real * degree_real - order_row * order_row, 1.0)
    )
    backward_gain = jnp.sqrt(
        jnp.maximum((degree_real - 1.0) ** 2 - order_row * order_row, 0.0)
        / jnp.maximum(4.0 * (degree_real - 1.0) ** 2 - 1.0, 1.0)
    )
    trig = jnp.concatenate(
        [
            jnp.cos(colatitude)[None, :],
            (math.pi / lat_count * sine_part)[None, :],
            seed_log,
        ],
        axis=0,
    )
    table = jax.ShapeDtypeStruct((order_share, degree_count, lat_count), jnp.bfloat16)
    smem = pl.BlockSpec(memory_space=pltpu.SMEM)
    vmem = pl.BlockSpec(memory_space=pltpu.VMEM)
    return pl.pallas_call(
        legendre_kernel,
        out_shape=(table, table),
        in_specs=[smem, smem, smem, vmem],
        out_specs=(vmem, vmem),
        name="legendre_tables",
    )(forward_gain, forward_gain * backward_gain, orders, trig)


def swap(blocks, axis):
    return lax.all_to_all(blocks, axis, split_axis=0, concat_axis=0, tiled=True)


def margin(blocks):
    return extended(blocks, (("lat", 1), ("lon", 2)), HW)


def analysis(field_blocks, dft_table, degree_table):
    partial = jnp.einsum(
        "ifc,fkjbe->jbekic", field_blocks, dft_table, preferred_element_type=jnp.float32
    ).astype(jnp.bfloat16)
    fourier = jnp.sum(swap(partial, "lon").astype(jnp.float32), axis=0).astype(jnp.bfloat16)
    columns = swap(fourier, "lat")
    degrees = jnp.einsum(
        "sekic,edlsi->dlekc", columns, degree_table, preferred_element_type=jnp.float32
    ).astype(jnp.bfloat16)
    return swap(degrees, "lat")


def synthesis(spectrum, degree_table, dft_table):
    by_degree = swap(spectrum, "lat")
    zonal_modes = jnp.einsum(
        "dlekc,edlsi->sekic", by_degree, degree_table, preferred_element_type=jnp.float32
    ).astype(jnp.bfloat16)
    by_order = swap(zonal_modes, "lat")
    lon_count = dft_table.shape[2]
    every = swap(jnp.broadcast_to(by_order[None], (lon_count,) + by_order.shape), "lon")
    return jnp.einsum(
        "jbekic,fkjbe->ifc", every, dft_table, preferred_element_type=jnp.float32
    ).astype(jnp.bfloat16)


def per_device(fields, cotangent, spectral_weight, local_weight, filter_basis, neighbor_rows):
    lat_count = lax.axis_size("lat")
    lon_count = lax.axis_size("lon")
    lat_index = lax.axis_index("lat")
    lon_index = lax.axis_index("lon")
    mem_count, lat_dev, lon_dev, channels = fields.shape
    degree_dev = spectral_weight.shape[0]
    kernel_count = filter_basis.shape[0]
    band_count = filter_basis.shape[2]
    support = filter_basis.shape[3]
    half_width = HW
    total_lat = lat_dev * lat_count
    total_lon = lon_dev * lon_count
    mode_dev = MDEV
    order_share = mode_dev // lat_count
    to_modes, from_modes = mode_tables(total_lon, mode_dev * lon_count)
    table_shape = (lon_dev, 2, lon_count, lat_count, order_share)
    to_modes = lax.dynamic_slice_in_dim(to_modes, lon_index * lon_dev, lon_dev, 0)
    from_modes = lax.dynamic_slice_in_dim(from_modes, lon_index * lon_dev, lon_dev, 0)
    to_modes = to_modes.reshape(table_shape)
    from_modes = from_modes.reshape(table_shape)
    orders = (
        lon_index * mode_dev + lat_index * order_share + jnp.arange(order_share, dtype=jnp.int32)
    )
    weighted, unweighted = legendre_tables(orders, degree_dev * lat_count, total_lat)
    degree_shape = (order_share, lat_count, degree_dev, lat_count, lat_dev)
    weighted = weighted.reshape(degree_shape)
    unweighted = unweighted.reshape(degree_shape)
    real_part = spectral_weight[:, 0]
    imag_part = spectral_weight[:, 1]
    complex_mix = jnp.stack(
        [jnp.stack([real_part, imag_part], axis=2), jnp.stack([-imag_part, real_part], axis=2)],
        axis=1,
    )
    harmonics = analysis(fields[0], to_modes, weighted)
    filtered = jnp.einsum(
        "bdekc,dkcjx->bdejx", harmonics, complex_mix, preferred_element_type=jnp.float32
    ).astype(jnp.bfloat16)
    spectral = synthesis(filtered, unweighted, from_modes)[None]
    padded = margin(fields)
    row_base = lat_index * lat_dev
    my_rows = lax.dynamic_slice_in_dim(neighbor_rows, row_base, lat_dev, 0)
    my_basis = lax.dynamic_slice_in_dim(filter_basis, row_base, lat_dev, 1)
    wide_count = lon_dev + 2 * half_width
    out_pos = jnp.arange(lon_dev, dtype=jnp.int32)[:, None, None]
    in_pos = jnp.arange(wide_count, dtype=jnp.int32)[None, :, None]
    tap_pos = jnp.arange(support, dtype=jnp.int32)[None, None, :]
    forward_pick = (in_pos - out_pos == tap_pos).astype(jnp.float32)
    local_sum = jnp.zeros((kernel_count, mem_count, lat_dev, lon_dev, channels), jnp.float32)
    for band_index in range(band_count):
        source_rows = my_rows[:, band_index] - row_base + half_width
        sources = jnp.take(padded, source_rows, axis=1)
        banded = jnp.einsum(
            "kis,fts->kift", my_basis[:, :, band_index, :].astype(jnp.float32), forward_pick
        ).astype(jnp.bfloat16)
        local_sum = local_sum + jnp.einsum(
            "kift,aitc->kaifc", banded, sources, preferred_element_type=jnp.float32
        )
    local_terms = local_sum.astype(jnp.bfloat16)
    pre_act = spectral.astype(jnp.float32) + jnp.einsum(
        "kaifc,kcd->aifd", local_terms, local_weight, preferred_element_type=jnp.float32
    )
    activation, derivative = gelu_parts(pre_act)
    block_output = (fields.astype(jnp.float32) + activation).astype(jnp.bfloat16)
    grad_mix = (cotangent.astype(jnp.float32) * derivative).astype(jnp.bfloat16)
    grad_filtered = analysis(grad_mix[0], from_modes, unweighted)
    grad_harmonics = jnp.einsum(
        "bdejx,dkcjx->bdekc", grad_filtered, complex_mix, preferred_element_type=jnp.float32
    ).astype(jnp.bfloat16)
    grad_spectral = synthesis(grad_harmonics, weighted, to_modes)[None]
    grad_padded = margin(grad_mix)
    grad_local = jnp.einsum(
        "aitd,kcd->kaitc", grad_padded, local_weight, preferred_element_type=jnp.float32
    ).astype(jnp.bfloat16)
    tall_count = lat_dev + 2 * half_width
    padded_rows = row_base - half_width + jnp.arange(tall_count, dtype=jnp.int32)
    inside = (padded_rows >= 0) & (padded_rows < total_lat)
    safe_rows = jnp.clip(padded_rows, 0, total_lat - 1)
    pad_neighbors = jnp.take(neighbor_rows, safe_rows, axis=0)
    pad_basis = jnp.take(filter_basis, safe_rows, axis=1)
    back_pick = (out_pos - in_pos + 2 * half_width == tap_pos).astype(jnp.float32)
    targets = jnp.arange(lat_dev, dtype=jnp.int32)
    grad_sum = jnp.zeros((mem_count, lat_dev, lon_dev, channels), jnp.float32)
    for band_index in range(band_count):
        banded = jnp.einsum(
            "kis,qts->kiqt", pad_basis[:, :, band_index, :].astype(jnp.float32), back_pick
        ).astype(jnp.bfloat16)
        spread = jnp.einsum(
            "kiqt,kaitc->aiqc", banded, grad_local, preferred_element_type=jnp.float32
        )
        placing = (
            (pad_neighbors[:, band_index][None, :] - row_base == targets[:, None]) & inside[None, :]
        ).astype(jnp.float32)
        grad_sum = grad_sum + jnp.einsum(
            "ji,aiqc->ajqc", placing, spread, precision=lax.Precision.HIGHEST
        )
    input_grad = (
        cotangent.astype(jnp.float32) + grad_spectral.astype(jnp.float32) + grad_sum
    ).astype(jnp.bfloat16)
    return (block_output, input_grad)


def solution(mesh):
    in_specs = (
        P(None, "lat", "lon", None),
        P(None, "lat", "lon", None),
        P("lat", None, None, None),
        P(),
        P(),
        P(),
    )
    out_specs = (P(None, "lat", "lon", None), P(None, "lat", "lon", None))
    return jax.shard_map(
        per_device, mesh=mesh, in_specs=in_specs, out_specs=out_specs, check_vma=False
    )
```

```python
import functools
import math

import jax
import jax.numpy as jnp
from jax import lax
from jax.experimental import pallas as pl
from jax.experimental.pallas import tpu as pltpu
from jax.sharding import PartitionSpec as P

MDEV = 16
HW = 8


TANH_SCALE = 0.7978845608028654
CUBIC_TERM = 0.044715


def extended(cells, sides, width):
    for axis, dim in sides:
        count = lax.axis_size(axis)
        head = lax.slice_in_dim(cells, 0, width, axis=dim)
        tail = lax.slice_in_dim(cells, cells.shape[dim] - width, cells.shape[dim], axis=dim)
        cells = jnp.concatenate(
            [
                lax.ppermute(tail, axis, [(i, (i + 1) % count) for i in range(count)]),
                cells,
                lax.ppermute(head, axis, [((i + 1) % count, i) for i in range(count)]),
            ],
            axis=dim,
        )
    return cells


def gelu_parts(values):
    tanh_input = TANH_SCALE * (values + CUBIC_TERM * values * values * values)
    hyper = jnp.tanh(tanh_input)
    result = 0.5 * values * (1.0 + hyper)
    derivative = 0.5 * (1.0 + hyper) + 0.5 * values * (1.0 - hyper * hyper) * TANH_SCALE * (
        1.0 + 3.0 * CUBIC_TERM * values * values
    )
    return (result, derivative)


def mode_tables(lon_count, mode_count):
    angles_int = (
        jnp.arange(lon_count, dtype=jnp.int32)[:, None]
        * jnp.arange(mode_count, dtype=jnp.int32)[None, :]
        % lon_count
    )
    angles = angles_int.astype(jnp.float32) * (2.0 * math.pi / lon_count)
    stacked = jnp.stack([jnp.cos(angles), -jnp.sin(angles)], axis=1)
    orders = jnp.arange(mode_count, dtype=jnp.int32)
    factor = jnp.where(orders == 0, 1.0, 2.0).astype(jnp.float32)
    to_modes = (stacked * (2.0 * math.pi / lon_count)).astype(jnp.bfloat16)
    from_modes = (stacked * factor[None, None, :]).astype(jnp.bfloat16)
    return (to_modes, from_modes)


STEP = 16


def legendre_kernel(gain_ref, back_ref, orders_ref, trig_ref, weighted_ref, plain_ref):
    order_share, degree_count, _ = plain_ref.shape
    cosine = trig_ref[0:1, :]
    quadrature = trig_ref[1:2, :]

    def block(index, state):
        carried = []
        for e in range(order_share):
            value, previous, log_scale = state[3 * e : 3 * e + 3]
            order = orders_ref[e]
            rows = []
            for step in range(STEP):
                degree = index * STEP + step
                active = degree > order
                following = gain_ref[e, degree] * (cosine * value) - back_ref[e, degree] * previous
                previous = jnp.where(active, value, previous)
                value = jnp.where(active, following, value)
                rows.append(jnp.where(degree >= order, value, 0.0))
            stacked = jnp.concatenate(rows, axis=0) * jnp.exp(log_scale)
            place = pl.ds(pl.multiple_of(index * STEP, STEP), STEP)
            plain_ref[e, place, :] = stacked.astype(jnp.bfloat16)
            weighted_ref[e, place, :] = (stacked * quadrature).astype(jnp.bfloat16)
            largest = jnp.maximum(jnp.abs(value), jnp.abs(previous))
            carried += [value / largest, previous / largest, log_scale + jnp.log(largest)]
        return tuple(carried)

    start = []
    for e in range(order_share):
        seed = trig_ref[2 + e : 3 + e, :]
        start += [jnp.ones_like(seed), jnp.zeros_like(seed), seed]
    lax.fori_loop(0, degree_count // STEP, block, tuple(start))


def legendre_tables(orders, degree_count, lat_count):
    order_share = orders.shape[0]
    colatitude = math.pi * (jnp.arange(lat_count, dtype=jnp.float32) + 0.5) / lat_count
    sine_part = jnp.sin(colatitude)
    order_real = orders.astype(jnp.float32)
    seed_log = 0.5 * (
        jnp.log((2.0 * order_real + 1.0) / (4.0 * math.pi))
        + lax.lgamma(order_real + 0.5)
        - lax.lgamma(order_real + 1.0)
        - 0.5 * math.log(math.pi)
    )
    seed_log = seed_log[:, None] + order_real[:, None] * jnp.log(sine_part)[None, :]
    degree_real = jnp.arange(degree_count, dtype=jnp.float32)[None, :]
    order_row = order_real[:, None]
    forward_gain = jnp.sqrt(
        jnp.maximum(4.0 * degree_real * degree_real - 1.0, 1.0)
        / jnp.maximum(degree_real * degree_real - order_row * order_row, 1.0)
    )
    backward_gain = jnp.sqrt(
        jnp.maximum((degree_real - 1.0) ** 2 - order_row * order_row, 0.0)
        / jnp.maximum(4.0 * (degree_real - 1.0) ** 2 - 1.0, 1.0)
    )
    trig = jnp.concatenate(
        [
            jnp.cos(colatitude)[None, :],
            (math.pi / lat_count * sine_part)[None, :],
            seed_log,
        ],
        axis=0,
    )
    table = jax.ShapeDtypeStruct((order_share, degree_count, lat_count), jnp.bfloat16)
    smem = pl.BlockSpec(memory_space=pltpu.SMEM)
    vmem = pl.BlockSpec(memory_space=pltpu.VMEM)
    return pl.pallas_call(
        legendre_kernel,
        out_shape=(table, table),
        in_specs=[smem, smem, smem, vmem],
        out_specs=(vmem, vmem),
        name="legendre_tables",
    )(forward_gain, forward_gain * backward_gain, orders, trig)


def margin(blocks):
    return extended(blocks, (("lat", 1), ("lon", 2)), HW)


def spectral_kernel(
    lat_count,
    lon_count,
    data_ref,
    first_ref,
    down_ref,
    up_ref,
    last_ref,
    mix_ref,
    out_ref,
    part_out,
    part_in,
    rows_out,
    rows_in,
    deg_out,
    deg_in,
    mixed_out,
    mixed_in,
    zonal_out,
    zonal_in,
    grid_out,
    grid_in,
    turned,
    blended,
    lon_send,
    lon_recv,
    lat_send,
    lat_recv,
):
    row_count, lon_dev, channels = data_ref.shape
    order_share = down_ref.shape[0]
    degree_dev = mix_ref.shape[0]
    wide = 2 * channels
    share = lat_count * order_share
    modes = 2 * share
    lat_me = lax.axis_index("lat")
    lon_me = lax.axis_index("lon")

    def others(me, count):
        return [lax.rem(me + step, count) for step in range(1, count)]

    barrier = pltpu.get_barrier_semaphore()
    for axis, me, count in (("lat", lat_me, lat_count), ("lon", lon_me, lon_count)):
        for peer in others(me, count):
            pl.semaphore_signal(
                barrier, inc=1, device_id={axis: peer}, device_id_type=pl.DeviceIdType.MESH
            )

    def exchange(axis, number, source, target, whole):
        me, count, send, recv = (
            (lat_me, lat_count, lat_send, lat_recv)
            if axis == "lat"
            else (lon_me, lon_count, lon_send, lon_recv)
        )
        copies = []
        for peer in others(me, count):
            copy = pltpu.make_async_remote_copy(
                src_ref=source if whole else source.at[peer],
                dst_ref=target.at[me],
                send_sem=send.at[number, peer],
                recv_sem=recv.at[number, me],
                device_id={axis: peer},
                device_id_type=pl.DeviceIdType.MESH,
            )
            copy.start()
            copies.append(copy)
        target[me] = source[...] if whole else source[me]
        for peer in others(me, count):
            pltpu.make_async_remote_copy(
                src_ref=source if whole else source.at[peer],
                dst_ref=target.at[peer],
                send_sem=send.at[number, peer],
                recv_sem=recv.at[number, peer],
                device_id={axis: peer},
                device_id_type=pl.DeviceIdType.MESH,
            ).wait_recv()
        for copy in copies:
            copy.wait_send()

    group = 8

    def transform(index, carry):
        for step in range(group):
            row = index * group + step
            part = jnp.dot(first_ref[...], data_ref[row], preferred_element_type=jnp.float32)
            part_out[:, row] = part.astype(jnp.bfloat16).reshape(lon_count, modes, channels)
        return carry

    lax.fori_loop(0, row_count // group, transform, 0)
    pl.semaphore_wait(barrier, lat_count + lon_count - 2)
    exchange("lon", 0, part_out, part_in, False)

    total = part_in[0].astype(jnp.float32)
    for sector in range(1, lon_count):
        total = total + part_in[sector].astype(jnp.float32)
    rows_out[...] = (
        jnp.swapaxes(total, 0, 1)
        .astype(jnp.bfloat16)
        .reshape(lat_count, order_share, 2, row_count, channels)
    )
    exchange("lat", 0, rows_out, rows_in, False)

    for e in range(order_share):
        columns = jnp.concatenate(
            [rows_in[:, e, part].reshape(lat_count * row_count, channels) for part in range(2)],
            axis=1,
        )
        degrees = jnp.dot(down_ref[e], columns, preferred_element_type=jnp.float32)
        deg_out[:, e] = degrees.astype(jnp.bfloat16).reshape(lat_count, degree_dev, wide)
    exchange("lat", 1, deg_out, deg_in, False)

    by_degree = deg_in[...].reshape(share, degree_dev, wide).astype(jnp.float32)
    turned[...] = jnp.swapaxes(by_degree, 0, 1).astype(jnp.bfloat16)

    def blend(index, carry):
        for step in range(group):
            degree = index * group + step
            pair = jnp.concatenate(
                [turned[degree, :, :channels], turned[degree, :, channels:]], axis=0
            )
            weights = jnp.concatenate([mix_ref[degree, 0], mix_ref[degree, 1]], axis=1)
            product = jnp.dot(pair, weights, preferred_element_type=jnp.float32)
            blended[degree, :, :channels] = product[:share, :channels] - product[share:, channels:]
            blended[degree, :, channels:] = product[:share, channels:] + product[share:, :channels]
        return carry

    lax.fori_loop(0, degree_dev // group, blend, 0)
    mixed_out[...] = (
        jnp.swapaxes(blended[...], 0, 1)
        .astype(jnp.bfloat16)
        .reshape(lat_count, order_share, degree_dev, wide)
    )
    exchange("lat", 2, mixed_out, mixed_in, False)

    for e in range(order_share):
        spectrum = mixed_in[:, e].reshape(lat_count * degree_dev, wide)
        zonal = lax.dot_general(
            up_ref[e], spectrum, (((0,), (0,)), ((), ())), preferred_element_type=jnp.float32
        ).astype(jnp.bfloat16)
        for part in range(2):
            zonal_out[:, e, part] = zonal[:, part * channels : (part + 1) * channels].reshape(
                lat_count, row_count, channels
            )
    exchange("lat", 3, zonal_out, zonal_in, False)

    by_order = zonal_in[...].reshape(modes, row_count, channels).astype(jnp.float32)
    grid_out[...] = jnp.swapaxes(by_order, 0, 1).astype(jnp.bfloat16)
    exchange("lon", 1, grid_out, grid_in, True)

    def restore(index, carry):
        for step in range(group):
            row = index * group + step
            every = grid_in[:, row].reshape(lon_count * modes, channels)
            out_ref[row] = jnp.dot(
                last_ref[...], every, preferred_element_type=jnp.float32
            ).astype(jnp.bfloat16)
        return carry

    lax.fori_loop(0, row_count // group, restore, 0)


def spectral_pass(lat_count, lon_count, data, first, down, up, last, mix):
    row_count, lon_dev, channels = data.shape
    order_share = down.shape[0]
    degree_dev = mix.shape[0]
    share = lat_count * order_share
    wide = 2 * channels
    bf16 = jnp.bfloat16
    part = pltpu.VMEM((lon_count, row_count, 2 * share, channels), bf16)
    rows = pltpu.VMEM((lat_count, order_share, 2, row_count, channels), bf16)
    degrees = pltpu.VMEM((lat_count, order_share, degree_dev, wide), bf16)
    vmem = pl.BlockSpec(memory_space=pltpu.VMEM)
    return pl.pallas_call(
        functools.partial(spectral_kernel, lat_count, lon_count),
        out_shape=jax.ShapeDtypeStruct(data.shape, bf16),
        in_specs=[vmem] * 6,
        out_specs=vmem,
        scratch_shapes=[
            part,
            part,
            rows,
            rows,
            degrees,
            degrees,
            degrees,
            degrees,
            rows,
            rows,
            pltpu.VMEM((row_count, 2 * share, channels), bf16),
            part,
            pltpu.VMEM((degree_dev, share, wide), bf16),
            pltpu.VMEM((degree_dev, share, wide), jnp.float32),
            pltpu.SemaphoreType.DMA((2, lon_count)),
            pltpu.SemaphoreType.DMA((2, lon_count)),
            pltpu.SemaphoreType.DMA((4, lat_count)),
            pltpu.SemaphoreType.DMA((4, lat_count)),
        ],
        compiler_params=pltpu.CompilerParams(
            collective_id=0, has_side_effects=True, vmem_limit_bytes=48 * 1024 * 1024
        ),
        name="spectral_pass",
    )(data, first, down, up, last, mix)


def per_device(fields, cotangent, spectral_weight, local_weight, filter_basis, neighbor_rows):
    lat_count = lax.axis_size("lat")
    lon_count = lax.axis_size("lon")
    lat_index = lax.axis_index("lat")
    lon_index = lax.axis_index("lon")
    mem_count, lat_dev, lon_dev, channels = fields.shape
    degree_dev = spectral_weight.shape[0]
    kernel_count = filter_basis.shape[0]
    band_count = filter_basis.shape[2]
    support = filter_basis.shape[3]
    half_width = HW
    total_lat = lat_dev * lat_count
    total_lon = lon_dev * lon_count
    mode_dev = MDEV
    order_share = mode_dev // lat_count
    to_modes, from_modes = mode_tables(total_lon, mode_dev * lon_count)
    table_shape = (lon_dev, 2, lon_count, lat_count, order_share)
    to_modes = lax.dynamic_slice_in_dim(to_modes, lon_index * lon_dev, lon_dev, 0)
    from_modes = lax.dynamic_slice_in_dim(from_modes, lon_index * lon_dev, lon_dev, 0)
    to_modes = to_modes.reshape(table_shape).transpose(0, 2, 3, 4, 1).reshape(lon_dev, -1)
    from_modes = from_modes.reshape(table_shape).transpose(0, 2, 3, 4, 1).reshape(lon_dev, -1)
    orders = (
        lon_index * mode_dev + lat_index * order_share + jnp.arange(order_share, dtype=jnp.int32)
    )
    weighted, unweighted = legendre_tables(orders, degree_dev * lat_count, total_lat)
    spectral = spectral_pass(
        lat_count, lon_count, fields[0], to_modes.T, weighted, unweighted, from_modes, spectral_weight
    )[None]
    padded = margin(fields)
    row_base = lat_index * lat_dev
    my_rows = lax.dynamic_slice_in_dim(neighbor_rows, row_base, lat_dev, 0)
    my_basis = lax.dynamic_slice_in_dim(filter_basis, row_base, lat_dev, 1)
    wide_count = lon_dev + 2 * half_width
    out_pos = jnp.arange(lon_dev, dtype=jnp.int32)[:, None, None]
    in_pos = jnp.arange(wide_count, dtype=jnp.int32)[None, :, None]
    tap_pos = jnp.arange(support, dtype=jnp.int32)[None, None, :]
    forward_pick = (in_pos - out_pos == tap_pos).astype(jnp.float32)
    local_sum = jnp.zeros((kernel_count, mem_count, lat_dev, lon_dev, channels), jnp.float32)
    for band_index in range(band_count):
        source_rows = my_rows[:, band_index] - row_base + half_width
        sources = jnp.take(padded, source_rows, axis=1)
        banded = jnp.einsum(
            "kis,fts->kift", my_basis[:, :, band_index, :].astype(jnp.float32), forward_pick
        ).astype(jnp.bfloat16)
        local_sum = local_sum + jnp.einsum(
            "kift,aitc->kaifc", banded, sources, preferred_element_type=jnp.float32
        )
    local_terms = local_sum.astype(jnp.bfloat16)
    pre_act = spectral.astype(jnp.float32) + jnp.einsum(
        "kaifc,kcd->aifd", local_terms, local_weight, preferred_element_type=jnp.float32
    )
    activation, derivative = gelu_parts(pre_act)
    block_output = (fields.astype(jnp.float32) + activation).astype(jnp.bfloat16)
    grad_mix = (cotangent.astype(jnp.float32) * derivative).astype(jnp.bfloat16)
    adjoint_mix = jnp.stack(
        [spectral_weight[:, 0].transpose(0, 2, 1), -spectral_weight[:, 1].transpose(0, 2, 1)], axis=1
    )
    grad_spectral = spectral_pass(
        lat_count, lon_count, grad_mix[0], from_modes.T, unweighted, weighted, to_modes, adjoint_mix
    )[None]
    grad_padded = margin(grad_mix)
    grad_local = jnp.einsum(
        "aitd,kcd->kaitc", grad_padded, local_weight, preferred_element_type=jnp.float32
    ).astype(jnp.bfloat16)
    tall_count = lat_dev + 2 * half_width
    padded_rows = row_base - half_width + jnp.arange(tall_count, dtype=jnp.int32)
    inside = (padded_rows >= 0) & (padded_rows < total_lat)
    safe_rows = jnp.clip(padded_rows, 0, total_lat - 1)
    pad_neighbors = jnp.take(neighbor_rows, safe_rows, axis=0)
    pad_basis = jnp.take(filter_basis, safe_rows, axis=1)
    back_pick = (out_pos - in_pos + 2 * half_width == tap_pos).astype(jnp.float32)
    targets = jnp.arange(lat_dev, dtype=jnp.int32)
    grad_sum = jnp.zeros((mem_count, lat_dev, lon_dev, channels), jnp.float32)
    for band_index in range(band_count):
        banded = jnp.einsum(
            "kis,qts->kiqt", pad_basis[:, :, band_index, :].astype(jnp.float32), back_pick
        ).astype(jnp.bfloat16)
        spread = jnp.einsum(
            "kiqt,kaitc->aiqc", banded, grad_local, preferred_element_type=jnp.float32
        )
        placing = (
            (pad_neighbors[:, band_index][None, :] - row_base == targets[:, None]) & inside[None, :]
        ).astype(jnp.float32)
        grad_sum = grad_sum + jnp.einsum(
            "ji,aiqc->ajqc", placing, spread, precision=lax.Precision.HIGHEST
        )
    input_grad = (
        cotangent.astype(jnp.float32) + grad_spectral.astype(jnp.float32) + grad_sum
    ).astype(jnp.bfloat16)
    return (block_output, input_grad)


def solution(mesh):
    in_specs = (
        P(None, "lat", "lon", None),
        P(None, "lat", "lon", None),
        P("lat", None, None, None),
        P(),
        P(),
        P(),
    )
    out_specs = (P(None, "lat", "lon", None), P(None, "lat", "lon", None))
    return jax.shard_map(
        per_device, mesh=mesh, in_specs=in_specs, out_specs=out_specs, check_vma=False
    )
```

```python
import functools
import math

import jax
import jax.numpy as jnp
from jax import lax
from jax.experimental import pallas as pl
from jax.experimental.pallas import tpu as pltpu
from jax.sharding import PartitionSpec as P

MDEV = 16
HW = 8


TANH_SCALE = 0.7978845608028654
CUBIC_TERM = 0.044715


def gelu_parts(values):
    tanh_input = TANH_SCALE * (values + CUBIC_TERM * values * values * values)
    hyper = jnp.tanh(tanh_input)
    result = 0.5 * values * (1.0 + hyper)
    derivative = 0.5 * (1.0 + hyper) + 0.5 * values * (1.0 - hyper * hyper) * TANH_SCALE * (
        1.0 + 3.0 * CUBIC_TERM * values * values
    )
    return (result, derivative)


def mode_tables(lon_count, mode_count):
    angles_int = (
        jnp.arange(lon_count, dtype=jnp.int32)[:, None]
        * jnp.arange(mode_count, dtype=jnp.int32)[None, :]
        % lon_count
    )
    angles = angles_int.astype(jnp.float32) * (2.0 * math.pi / lon_count)
    stacked = jnp.stack([jnp.cos(angles), -jnp.sin(angles)], axis=1)
    orders = jnp.arange(mode_count, dtype=jnp.int32)
    factor = jnp.where(orders == 0, 1.0, 2.0).astype(jnp.float32)
    to_modes = (stacked * (2.0 * math.pi / lon_count)).astype(jnp.bfloat16)
    from_modes = (stacked * factor[None, None, :]).astype(jnp.bfloat16)
    return (to_modes, from_modes)


STEP = 16


def legendre_kernel(gain_ref, back_ref, orders_ref, trig_ref, weighted_ref, plain_ref):
    order_share, degree_count, _ = plain_ref.shape
    cosine = trig_ref[0:1, :]
    quadrature = trig_ref[1:2, :]

    def block(index, state):
        carried = []
        for e in range(order_share):
            value, previous, log_scale = state[3 * e : 3 * e + 3]
            order = orders_ref[e]
            rows = []
            for step in range(STEP):
                degree = index * STEP + step
                active = degree > order
                following = gain_ref[e, degree] * (cosine * value) - back_ref[e, degree] * previous
                previous = jnp.where(active, value, previous)
                value = jnp.where(active, following, value)
                rows.append(jnp.where(degree >= order, value, 0.0))
            stacked = jnp.concatenate(rows, axis=0) * jnp.exp(log_scale)
            place = pl.ds(pl.multiple_of(index * STEP, STEP), STEP)
            plain_ref[e, place, :] = stacked.astype(jnp.bfloat16)
            weighted_ref[e, place, :] = (stacked * quadrature).astype(jnp.bfloat16)
            largest = jnp.maximum(jnp.abs(value), jnp.abs(previous))
            carried += [value / largest, previous / largest, log_scale + jnp.log(largest)]
        return tuple(carried)

    start = []
    for e in range(order_share):
        seed = trig_ref[2 + e : 3 + e, :]
        start += [jnp.ones_like(seed), jnp.zeros_like(seed), seed]
    lax.fori_loop(0, degree_count // STEP, block, tuple(start))


def legendre_tables(orders, degree_count, lat_count):
    order_share = orders.shape[0]
    colatitude = math.pi * (jnp.arange(lat_count, dtype=jnp.float32) + 0.5) / lat_count
    sine_part = jnp.sin(colatitude)
    order_real = orders.astype(jnp.float32)
    seed_log = 0.5 * (
        jnp.log((2.0 * order_real + 1.0) / (4.0 * math.pi))
        + lax.lgamma(order_real + 0.5)
        - lax.lgamma(order_real + 1.0)
        - 0.5 * math.log(math.pi)
    )
    seed_log = seed_log[:, None] + order_real[:, None] * jnp.log(sine_part)[None, :]
    degree_real = jnp.arange(degree_count, dtype=jnp.float32)[None, :]
    order_row = order_real[:, None]
    forward_gain = jnp.sqrt(
        jnp.maximum(4.0 * degree_real * degree_real - 1.0, 1.0)
        / jnp.maximum(degree_real * degree_real - order_row * order_row, 1.0)
    )
    backward_gain = jnp.sqrt(
        jnp.maximum((degree_real - 1.0) ** 2 - order_row * order_row, 0.0)
        / jnp.maximum(4.0 * (degree_real - 1.0) ** 2 - 1.0, 1.0)
    )
    trig = jnp.concatenate(
        [
            jnp.cos(colatitude)[None, :],
            (math.pi / lat_count * sine_part)[None, :],
            seed_log,
        ],
        axis=0,
    )
    table = jax.ShapeDtypeStruct((order_share, degree_count, lat_count), jnp.bfloat16)
    smem = pl.BlockSpec(memory_space=pltpu.SMEM)
    vmem = pl.BlockSpec(memory_space=pltpu.VMEM)
    return pl.pallas_call(
        legendre_kernel,
        out_shape=(table, table),
        in_specs=[smem, smem, smem, vmem],
        out_specs=(vmem, vmem),
        name="legendre_tables",
    )(forward_gain, forward_gain * backward_gain, orders, trig)


CHUNKS = 2
EDGE = 2 * HW


def spectral_kernel(
    lat_count,
    lon_count,
    adjoint,
    data_ref,
    first_ref,
    down_ref,
    up_ref,
    last_ref,
    mix_ref,
    out_ref,
    padded_ref,
    part_out,
    pair_in,
    pair_out,
    cross_in,
    rows_out,
    rows_in,
    deg_out,
    deg_in,
    mixed_out,
    mixed_in,
    zonal_out,
    zonal_in,
    grid_out,
    grid_in,
    blended,
    pair_sems,
    cross_sems,
    lat_sems,
    gather_sems,
    relay_sems,
    halo_sems,
):
    row_count, lon_dev, channels = data_ref.shape
    order_share = down_ref.shape[0]
    degree_dev = mix_ref.shape[0]
    wide = 2 * channels
    share = lat_count * order_share
    modes = 2 * share
    chips = lon_count // 2
    rows_each = row_count // CHUNKS
    degrees_each = degree_dev // CHUNKS
    lat_me = lax.axis_index("lat")
    lon_me = lax.axis_index("lon")
    chip = lon_me // 2
    core = lax.rem(lon_me, 2)
    mate = 2 * chip + 1 - core
    lat_peers = [lax.rem(lat_me + step, lat_count) for step in range(1, lat_count)]
    chip_peers = [lax.rem(chip + step, chips) for step in range(1, chips)]
    lat_next = lax.rem(lat_me + 1, lat_count)
    lat_last = lax.rem(lat_me + lat_count - 1, lat_count)
    lon_next = lax.rem(lon_me + 1, lon_count)
    lon_last = lax.rem(lon_me + lon_count - 1, lon_count)
    halo_rows = {
        0: (lat_me, slice(0, row_count), slice(HW, HW + row_count)),
        1: (lat_next, slice(row_count - HW, row_count), slice(0, HW)),
        2: (lat_last, slice(0, HW), slice(HW + row_count, 2 * HW + row_count)),
    }
    halo_columns = {
        0: (lon_me, slice(0, lon_dev), slice(EDGE, EDGE + lon_dev)),
        1: (lon_next, slice(lon_dev - EDGE, lon_dev), slice(0, EDGE)),
        2: (lon_last, slice(0, EDGE), slice(EDGE + lon_dev, 2 * EDGE + lon_dev)),
    }

    barrier = pltpu.get_barrier_semaphore()

    def greet(lat, lon):
        pl.semaphore_signal(
            barrier, inc=1, device_id=(lat, lon), device_id_type=pl.DeviceIdType.MESH
        )

    for peer in lat_peers:
        greet(peer, lon_me)
    for step in range(1, lon_count):
        greet(lat_me, lax.rem(lon_me + step, lon_count))
    for lat in (lat_next, lat_last):
        for lon in (lon_next, lon_last):
            greet(lat, lon)
    greetings = lat_count - 1 + lon_count - 1 + 4

    started = []

    def copying(source, target, sems, place, came, device):
        return pltpu.make_async_remote_copy(
            src_ref=source,
            dst_ref=target,
            send_sem=sems.at[(0,) + place],
            recv_sem=sems.at[(1,) + came],
            device_id=device,
            device_id_type=pl.DeviceIdType.MESH,
        )

    def push(source, target, sems, place, came, device):
        copy = copying(source, target, sems, place, came, device)
        copy.start()
        started.append(copy)

    def arrived(target, sems, came):
        copying(target, target, sems, came, came, (lat_me, mate)).wait_recv()

    def rows_of(number):
        return pl.ds(number * rows_each, rows_each)

    def transform(number):
        group = 8

        def body(index, carry):
            for step in range(group):
                row = number * rows_each + index * group + step
                part = jnp.dot(
                    first_ref[...], data_ref[row], preferred_element_type=jnp.float32
                ).astype(jnp.bfloat16)
                for other in range(chips):
                    for side in range(2):
                        begin = (2 * other + side) * modes
                        part_out[side, other, row] = part[begin : begin + modes]
            return carry

        lax.fori_loop(0, rows_each // group, body, 0)

    def lat_push(number, piece, source, target):
        for peer in lat_peers:
            push(
                source(peer),
                target(lat_me),
                lat_sems,
                (number, piece, peer),
                (number, piece, lat_me),
                (peer, lon_me),
            )

    def lat_arrived(number, piece, target):
        for peer in lat_peers:
            arrived(target(peer), lat_sems, (number, piece, peer))

    for number in range(CHUNKS):
        transform(number)
        if number == 0:
            pl.semaphore_wait(barrier, greetings)
        push(
            part_out.at[1 - core, :, rows_of(number)],
            pair_in.at[:, rows_of(number)],
            pair_sems,
            (number,),
            (number,),
            (lat_me, mate),
        )
    for r, (lat, from_rows, to_rows) in halo_rows.items():
        for c, (lon, from_columns, to_columns) in halo_columns.items():
            if r or c:
                push(
                    data_ref.at[from_rows, from_columns],
                    padded_ref.at[to_rows, to_columns],
                    halo_sems,
                    (3 * r + c,),
                    (3 * r + c,),
                    (lat, lon),
                )
    for number in range(CHUNKS):
        piece = rows_of(number)
        arrived(pair_in.at[:, piece], pair_sems, (number,))
        for other in chip_peers:
            pair_out[other, piece] = (
                part_out[core, other, piece].astype(jnp.float32)
                + pair_in[other, piece].astype(jnp.float32)
            ).astype(jnp.bfloat16)
            push(
                pair_out.at[other, piece],
                cross_in.at[chip, piece],
                cross_sems,
                (number, other),
                (number, chip),
                (lat_me, 2 * other + core),
            )
    padded_ref[HW : HW + row_count, EDGE : EDGE + lon_dev] = data_ref[...]
    for number in range(CHUNKS):
        piece = rows_of(number)
        total = part_out[core, chip, piece].astype(jnp.float32) + pair_in[chip, piece].astype(
            jnp.float32
        )
        for other in chip_peers:
            arrived(cross_in.at[other, piece], cross_sems, (number, other))
            total = total + cross_in[other, piece].astype(jnp.float32)
        begin = number * rows_each
        rows_out[:, :, :, begin : begin + rows_each] = (
            jnp.swapaxes(total, 0, 1)
            .astype(jnp.bfloat16)
            .reshape(lat_count, order_share, 2, rows_each, channels)
        )
        lat_push(
            0,
            number,
            lambda peer: rows_out.at[peer, :, :, piece],
            lambda peer: rows_in.at[peer, :, :, piece],
        )
    rows_in[lat_me] = rows_out[lat_me]
    for number in range(CHUNKS):
        piece = rows_of(number)
        lat_arrived(0, number, lambda peer: rows_in.at[peer, :, :, piece])

    for e in range(order_share):
        columns = jnp.concatenate(
            [rows_in[:, e, part].reshape(lat_count * row_count, channels) for part in range(2)],
            axis=1,
        )
        degrees = jnp.dot(down_ref[e], columns, preferred_element_type=jnp.float32)
        deg_out[:, e] = degrees.astype(jnp.bfloat16).reshape(lat_count, degree_dev, wide)
    for number in range(CHUNKS):
        piece = pl.ds(number * degrees_each, degrees_each)
        lat_push(
            1,
            number,
            lambda peer: deg_out.at[peer, :, piece],
            lambda peer: deg_in.at[peer, :, piece],
        )
    deg_in[lat_me] = deg_out[lat_me]

    for number in range(CHUNKS):
        begin = number * degrees_each
        piece = pl.ds(begin, degrees_each)
        lat_arrived(1, number, lambda peer: deg_in.at[peer, :, piece])
        by_degree = deg_in[:, :, begin : begin + degrees_each].reshape(share, degrees_each, wide)
        turned = jnp.swapaxes(by_degree.astype(jnp.float32), 0, 1).astype(jnp.bfloat16)
        for step in range(degrees_each):
            degree = begin + step
            pair = jnp.concatenate([turned[step, :, :channels], turned[step, :, channels:]], axis=0)
            if adjoint:
                weights = jnp.concatenate([mix_ref[degree, 0], mix_ref[degree, 1]], axis=0)
                product = lax.dot_general(
                    pair, weights, (((1,), (1,)), ((), ())), preferred_element_type=jnp.float32
                )
            else:
                weights = jnp.concatenate([mix_ref[degree, 0], mix_ref[degree, 1]], axis=1)
                product = jnp.dot(pair, weights, preferred_element_type=jnp.float32)
            sign = -1.0 if adjoint else 1.0
            blended[step, :, :channels] = (
                product[:share, :channels] - sign * product[share:, channels:]
            )
            blended[step, :, channels:] = (
                sign * product[:share, channels:] + product[share:, :channels]
            )
        mixed_out[:, :, begin : begin + degrees_each] = (
            jnp.swapaxes(blended[...], 0, 1)
            .astype(jnp.bfloat16)
            .reshape(lat_count, order_share, degrees_each, wide)
        )
        lat_push(
            2,
            number,
            lambda peer: mixed_out.at[peer, :, piece],
            lambda peer: mixed_in.at[peer, :, piece],
        )
    mixed_in[lat_me] = mixed_out[lat_me]
    for number in range(CHUNKS):
        piece = pl.ds(number * degrees_each, degrees_each)
        lat_arrived(2, number, lambda peer: mixed_in.at[peer, :, piece])

    for e in range(order_share):
        spectrum = mixed_in[:, e].reshape(lat_count * degree_dev, wide)
        zonal = lax.dot_general(
            up_ref[e], spectrum, (((0,), (0,)), ((), ())), preferred_element_type=jnp.float32
        ).astype(jnp.bfloat16)
        for part in range(2):
            zonal_out[:, e, part] = zonal[:, part * channels : (part + 1) * channels].reshape(
                lat_count, row_count, channels
            )
    for number in range(CHUNKS):
        piece = rows_of(number)
        lat_push(
            3,
            number,
            lambda peer: zonal_out.at[peer, :, :, piece],
            lambda peer: zonal_in.at[peer, :, :, piece],
        )
    zonal_in[lat_me] = zonal_out[lat_me]

    for number in range(CHUNKS):
        piece = rows_of(number)
        begin = number * rows_each
        lat_arrived(3, number, lambda peer: zonal_in.at[peer, :, :, piece])
        by_order = zonal_in[:, :, :, begin : begin + rows_each].reshape(modes, rows_each, channels)
        grid_out[piece] = jnp.swapaxes(by_order.astype(jnp.float32), 0, 1).astype(jnp.bfloat16)
        for lon in [2 * other + core for other in chip_peers] + [mate]:
            push(
                grid_out.at[piece],
                grid_in.at[lon_me, piece],
                gather_sems,
                (number, lon),
                (number, lon_me),
                (lat_me, lon),
            )
        grid_in[lon_me, piece] = grid_out[piece]
    for number in range(CHUNKS):
        piece = rows_of(number)
        for other in chip_peers:
            slot = 2 * other + core
            arrived(grid_in.at[slot, piece], gather_sems, (number, slot))
            push(
                grid_in.at[slot, piece],
                grid_in.at[slot, piece],
                relay_sems,
                (number, slot),
                (number, slot),
                (lat_me, mate),
            )
    for number in range(CHUNKS):
        piece = rows_of(number)
        arrived(grid_in.at[mate, piece], gather_sems, (number, mate))
        for other in chip_peers:
            slot = 2 * other + 1 - core
            arrived(grid_in.at[slot, piece], relay_sems, (number, slot))

        def restore(index, carry):
            for step in range(8):
                row = number * rows_each + index * 8 + step
                every = grid_in[:, row].reshape(lon_count * modes, channels)
                out_ref[row] = jnp.dot(
                    last_ref[...], every, preferred_element_type=jnp.float32
                ).astype(jnp.bfloat16)
            return carry

        lax.fori_loop(0, rows_each // 8, restore, 0)

    for r, (lat, from_rows, to_rows) in halo_rows.items():
        for c, (lon, from_columns, to_columns) in halo_columns.items():
            if r or c:
                arrived(padded_ref.at[to_rows, to_columns], halo_sems, (3 * r + c,))
    for copy in started:
        copy.wait_send()


def spectral_pass(lat_count, lon_count, adjoint, data, first, down, up, last, mix):
    row_count, lon_dev, channels = data.shape
    order_share = down.shape[0]
    degree_dev = mix.shape[0]
    share = lat_count * order_share
    wide = 2 * channels
    chips = lon_count // 2
    bf16 = jnp.bfloat16
    part = pltpu.VMEM((chips, row_count, 2 * share, channels), bf16)
    rows = pltpu.VMEM((lat_count, order_share, 2, row_count, channels), bf16)
    degrees = pltpu.VMEM((lat_count, order_share, degree_dev, wide), bf16)
    vmem = pl.BlockSpec(memory_space=pltpu.VMEM)
    return pl.pallas_call(
        functools.partial(spectral_kernel, lat_count, lon_count, adjoint),
        out_shape=(
            jax.ShapeDtypeStruct(data.shape, bf16),
            jax.ShapeDtypeStruct((row_count + 2 * HW, lon_dev + 2 * EDGE, channels), bf16),
        ),
        in_specs=[vmem] * 6,
        out_specs=(vmem, vmem),
        scratch_shapes=[
            pltpu.VMEM((2, chips, row_count, 2 * share, channels), bf16),
            part,
            part,
            part,
            rows,
            rows,
            degrees,
            degrees,
            degrees,
            degrees,
            rows,
            rows,
            pltpu.VMEM((row_count, 2 * share, channels), bf16),
            pltpu.VMEM((lon_count, row_count, 2 * share, channels), bf16),
            pltpu.VMEM((degree_dev // CHUNKS, share, wide), jnp.float32),
            pltpu.SemaphoreType.DMA((2, CHUNKS)),
            pltpu.SemaphoreType.DMA((2, CHUNKS, chips)),
            pltpu.SemaphoreType.DMA((2, 4, CHUNKS, lat_count)),
            pltpu.SemaphoreType.DMA((2, CHUNKS, lon_count)),
            pltpu.SemaphoreType.DMA((2, CHUNKS, lon_count)),
            pltpu.SemaphoreType.DMA((2, 9)),
        ],
        compiler_params=pltpu.CompilerParams(
            collective_id=1 if adjoint else 0,
            has_side_effects=True,
            vmem_limit_bytes=48 * 1024 * 1024,
        ),
        name="spectral_adjoint" if adjoint else "spectral_forward",
    )(data, first, down, up, last, mix)


def toeplitz(taps, count):
    spread = [
        pltpu.roll(
            jnp.broadcast_to(taps[k : k + 1, :], (count, taps.shape[1])),
            0,
            1,
            stride=1,
            stride_axis=0,
        )
        for k in range(taps.shape[0])
    ]
    return jnp.concatenate(spread, axis=0).astype(jnp.bfloat16)


def stretch(padded_ref, whole_ref):
    width = whole_ref.shape[1]

    def body(row, carry):
        whole_ref[row] = padded_ref[row].astype(jnp.float32)[HW : HW + width]
        return carry

    lax.fori_loop(0, whole_ref.shape[0], body, 0)


def local_kernel(
    rows_ref, taps_ref, padded_ref, spectral_ref, cotangent_ref, weight_ref, out_ref, mix_ref, whole
):
    row_count, lon_dev, channels = out_ref.shape
    width = whole.shape[1]
    kernel_count = taps_ref.shape[1]
    band_count = rows_ref.shape[1]
    stretch(padded_ref, whole)
    spare = jnp.zeros((taps_ref.shape[2] - band_count * width, channels), jnp.float32)

    def one(row):
        sources = jnp.concatenate(
            [whole[rows_ref[row, band]] for band in range(band_count)] + [spare], axis=0
        ).astype(jnp.bfloat16)
        terms = jnp.dot(
            toeplitz(taps_ref[row], lon_dev), sources, preferred_element_type=jnp.float32
        ).astype(jnp.bfloat16)
        flat = jnp.concatenate(
            [terms[k * lon_dev : (k + 1) * lon_dev] for k in range(kernel_count)], axis=1
        )
        pre_act = spectral_ref[row].astype(jnp.float32) + jnp.dot(
            flat, weight_ref[...], preferred_element_type=jnp.float32
        )
        activation, derivative = gelu_parts(pre_act)
        field = whole[row + HW][HW : HW + lon_dev]
        out_ref[row] = (field + activation).astype(jnp.bfloat16)
        mix_ref[row] = (cotangent_ref[row].astype(jnp.float32) * derivative).astype(jnp.bfloat16)

    def body(index, carry):
        for step in range(4):
            one(4 * index + step)
        return carry

    lax.fori_loop(0, row_count // 4, body, 0)


def local_adjoint_kernel(
    rows_ref, taps_ref, padded_ref, spectral_ref, cotangent_ref, weight_ref, out_ref, whole, total
):
    row_count, lon_dev, channels = out_ref.shape
    tall, width, _ = whole.shape
    band_count = rows_ref.shape[1]
    kernel_count = weight_ref.shape[1] // channels
    stretch(padded_ref, whole)
    spare = jnp.zeros((taps_ref.shape[2] - kernel_count * width, channels), jnp.bfloat16)
    total[...] = jnp.zeros_like(total)

    def body(index, carry):
        pieces = []
        for step in range(4):
            row = 4 * index + step
            grads = jnp.dot(
                whole[row].astype(jnp.bfloat16), weight_ref[...], preferred_element_type=jnp.float32
            ).astype(jnp.bfloat16)
            stacked = jnp.concatenate(
                [grads[:, k * channels : (k + 1) * channels] for k in range(kernel_count)] + [spare],
                axis=0,
            )
            pieces.append(
                jnp.dot(
                    toeplitz(taps_ref[row], lon_dev), stacked, preferred_element_type=jnp.float32
                )
            )
        for step in range(4):
            for band in range(band_count):
                target = rows_ref[4 * index + step, band]
                total[target] += pieces[step][band * lon_dev : (band + 1) * lon_dev]
        return carry

    lax.fori_loop(0, tall // 4, body, 0)
    out_ref[...] = (
        cotangent_ref[...].astype(jnp.float32)
        + spectral_ref[...].astype(jnp.float32)
        + total[2 * HW : 2 * HW + row_count]
    ).astype(jnp.bfloat16)


def tap_rows(basis, width):
    flat = jnp.pad(basis, ((0, 0), (0, 0), (0, 0), (0, width - basis.shape[3])))
    flat = flat.reshape(basis.shape[0], basis.shape[1], basis.shape[2] * width)
    lanes = -(-flat.shape[2] // 128) * 128
    return jnp.pad(flat, ((0, 0), (0, 0), (0, lanes - flat.shape[2]))).astype(jnp.float32)


def per_device(fields, cotangent, spectral_weight, local_weight, filter_basis, neighbor_rows):
    lat_count = lax.axis_size("lat")
    lon_count = lax.axis_size("lon")
    lat_index = lax.axis_index("lat")
    lon_index = lax.axis_index("lon")
    _, lat_dev, lon_dev, channels = fields.shape
    degree_dev = spectral_weight.shape[0]
    kernel_count = filter_basis.shape[0]
    total_lat = lat_dev * lat_count
    total_lon = lon_dev * lon_count
    order_share = MDEV // lat_count
    width = lon_dev + 2 * HW
    tall = lat_dev + 2 * HW
    to_modes, from_modes = mode_tables(total_lon, MDEV * lon_count)
    table_shape = (lon_dev, 2, lon_count, lat_count, order_share)
    to_modes = lax.dynamic_slice_in_dim(to_modes, lon_index * lon_dev, lon_dev, 0)
    from_modes = lax.dynamic_slice_in_dim(from_modes, lon_index * lon_dev, lon_dev, 0)
    to_modes = to_modes.reshape(table_shape).transpose(0, 2, 3, 4, 1).reshape(lon_dev, -1)
    from_modes = from_modes.reshape(table_shape).transpose(0, 2, 3, 4, 1).reshape(lon_dev, -1)
    orders = (
        lon_index * MDEV + lat_index * order_share + jnp.arange(order_share, dtype=jnp.int32)
    )
    weighted, unweighted = legendre_tables(orders, degree_dev * lat_count, total_lat)
    row_base = lat_index * lat_dev
    near_rows = lax.dynamic_slice_in_dim(
        jnp.pad(neighbor_rows, ((HW, HW), (0, 0))), row_base, tall, 0
    )
    near_basis = lax.dynamic_slice_in_dim(
        jnp.pad(filter_basis, ((0, 0), (HW, HW), (0, 0), (0, 0))), row_base, tall, 1
    )
    sources = near_rows[HW : HW + lat_dev] - row_base + HW
    targets = jnp.clip(near_rows - row_base + 2 * HW, 0, lat_dev + 4 * HW - 1)
    taps = tap_rows(near_basis[:, HW : HW + lat_dev].transpose(1, 0, 2, 3), width)
    back_taps = tap_rows(near_basis[..., ::-1].transpose(1, 2, 0, 3), width)
    smem = pl.BlockSpec(memory_space=pltpu.SMEM)
    vmem = pl.BlockSpec(memory_space=pltpu.VMEM)
    grid = jax.ShapeDtypeStruct((lat_dev, lon_dev, channels), jnp.bfloat16)
    whole = pltpu.VMEM((tall, width, channels), jnp.float32)
    params = pltpu.CompilerParams(vmem_limit_bytes=40 * 1024 * 1024)

    spectral, padded = spectral_pass(
        lat_count,
        lon_count,
        False,
        fields[0],
        to_modes.T,
        weighted,
        unweighted,
        from_modes,
        spectral_weight,
    )
    block_output, grad_mix = pl.pallas_call(
        local_kernel,
        out_shape=(grid, grid),
        in_specs=[smem] + [vmem] * 5,
        out_specs=(vmem, vmem),
        scratch_shapes=[whole],
        compiler_params=params,
        name="local_forward",
    )(sources, taps, padded, spectral, cotangent[0], local_weight.reshape(-1, channels))
    grad_spectral, grad_padded = spectral_pass(
        lat_count,
        lon_count,
        True,
        grad_mix,
        from_modes.T,
        unweighted,
        weighted,
        to_modes,
        spectral_weight,
    )
    input_grad = pl.pallas_call(
        local_adjoint_kernel,
        out_shape=grid,
        in_specs=[smem] + [vmem] * 5,
        out_specs=vmem,
        scratch_shapes=[whole, pltpu.VMEM((lat_dev + 4 * HW, lon_dev, channels), jnp.float32)],
        compiler_params=params,
        name="local_adjoint",
    )(
        targets,
        back_taps,
        grad_padded,
        grad_spectral,
        cotangent[0],
        local_weight.transpose(2, 0, 1).reshape(channels, kernel_count * channels),
    )
    return (block_output[None], input_grad[None])


def solution(mesh):
    in_specs = (
        P(None, "lat", "lon", None),
        P(None, "lat", "lon", None),
        P("lat", None, None, None),
        P(),
        P(),
        P(),
    )
    out_specs = (P(None, "lat", "lon", None), P(None, "lat", "lon", None))
    return jax.shard_map(
        per_device, mesh=mesh, in_specs=in_specs, out_specs=out_specs, check_vma=False
    )
```

```python
import functools
import math

import jax
import jax.numpy as jnp
from jax import lax
from jax.experimental import pallas as pl
from jax.experimental.pallas import tpu as pltpu
from jax.sharding import PartitionSpec as P

MDEV = 16
HW = 8


TANH_SCALE = 0.7978845608028654
CUBIC_TERM = 0.044715


def gelu_parts(values):
    tanh_input = TANH_SCALE * (values + CUBIC_TERM * values * values * values)
    hyper = jnp.tanh(tanh_input)
    result = 0.5 * values * (1.0 + hyper)
    derivative = 0.5 * (1.0 + hyper) + 0.5 * values * (1.0 - hyper * hyper) * TANH_SCALE * (
        1.0 + 3.0 * CUBIC_TERM * values * values
    )
    return (result, derivative)


def mode_tables(lon_count, mode_count):
    angles_int = (
        jnp.arange(lon_count, dtype=jnp.int32)[:, None]
        * jnp.arange(mode_count, dtype=jnp.int32)[None, :]
        % lon_count
    )
    angles = angles_int.astype(jnp.float32) * (2.0 * math.pi / lon_count)
    stacked = jnp.stack([jnp.cos(angles), -jnp.sin(angles)], axis=1)
    orders = jnp.arange(mode_count, dtype=jnp.int32)
    factor = jnp.where(orders == 0, 1.0, 2.0).astype(jnp.float32)
    to_modes = (stacked * (2.0 * math.pi / lon_count)).astype(jnp.bfloat16)
    from_modes = (stacked * factor[None, None, :]).astype(jnp.bfloat16)
    return (to_modes, from_modes)


STEP = 16


def legendre_kernel(gain_ref, back_ref, orders_ref, trig_ref, weighted_ref, plain_ref):
    order_share, degree_count, _ = plain_ref.shape
    cosine = trig_ref[0:1, :]
    quadrature = trig_ref[1:2, :]

    def block(index, state):
        carried = []
        for e in range(order_share):
            value, previous, log_scale = state[3 * e : 3 * e + 3]
            order = orders_ref[e]
            rows = []
            for step in range(STEP):
                degree = index * STEP + step
                active = degree > order
                following = gain_ref[e, degree] * (cosine * value) - back_ref[e, degree] * previous
                previous = jnp.where(active, value, previous)
                value = jnp.where(active, following, value)
                rows.append(jnp.where(degree >= order, value, 0.0))
            stacked = jnp.concatenate(rows, axis=0) * jnp.exp(log_scale)
            place = pl.ds(pl.multiple_of(index * STEP, STEP), STEP)
            plain_ref[e, place, :] = stacked.astype(jnp.bfloat16)
            weighted_ref[e, place, :] = (stacked * quadrature).astype(jnp.bfloat16)
            largest = jnp.maximum(jnp.abs(value), jnp.abs(previous))
            carried += [value / largest, previous / largest, log_scale + jnp.log(largest)]
        return tuple(carried)

    start = []
    for e in range(order_share):
        seed = trig_ref[2 + e : 3 + e, :]
        start += [jnp.ones_like(seed), jnp.zeros_like(seed), seed]
    lax.fori_loop(0, degree_count // STEP, block, tuple(start))


def legendre_inputs(orders, degree_count, lat_count):
    order_share = orders.shape[0]
    colatitude = math.pi * (jnp.arange(lat_count, dtype=jnp.float32) + 0.5) / lat_count
    sine_part = jnp.sin(colatitude)
    order_real = orders.astype(jnp.float32)
    seed_log = 0.5 * (
        jnp.log((2.0 * order_real + 1.0) / (4.0 * math.pi))
        + lax.lgamma(order_real + 0.5)
        - lax.lgamma(order_real + 1.0)
        - 0.5 * math.log(math.pi)
    )
    seed_log = seed_log[:, None] + order_real[:, None] * jnp.log(sine_part)[None, :]
    degree_real = jnp.arange(degree_count, dtype=jnp.float32)[None, :]
    order_row = order_real[:, None]
    forward_gain = jnp.sqrt(
        jnp.maximum(4.0 * degree_real * degree_real - 1.0, 1.0)
        / jnp.maximum(degree_real * degree_real - order_row * order_row, 1.0)
    )
    backward_gain = jnp.sqrt(
        jnp.maximum((degree_real - 1.0) ** 2 - order_row * order_row, 0.0)
        / jnp.maximum(4.0 * (degree_real - 1.0) ** 2 - 1.0, 1.0)
    )
    trig = jnp.concatenate(
        [
            jnp.cos(colatitude)[None, :],
            (math.pi / lat_count * sine_part)[None, :],
            seed_log,
        ],
        axis=0,
    )
    return (forward_gain, forward_gain * backward_gain, trig)


CHUNKS = 2
EDGE = 2 * HW


def place_of(lat_count, lon_count):
    lat_me = lax.axis_index("lat")
    lon_me = lax.axis_index("lon")
    return lat_me, lon_me


def enter(lat_count, lon_count):
    lat_me, lon_me = place_of(lat_count, lon_count)
    barrier = pltpu.get_barrier_semaphore()

    def greet(lat, lon):
        pl.semaphore_signal(
            barrier, inc=1, device_id=(lat, lon), device_id_type=pl.DeviceIdType.MESH
        )

    for step in range(1, lat_count):
        greet(lax.rem(lat_me + step, lat_count), lon_me)
    for step in range(1, lon_count):
        greet(lat_me, lax.rem(lon_me + step, lon_count))
    for lat_step in (1, lat_count - 1):
        for lon_step in (1, lon_count - 1):
            greet(lax.rem(lat_me + lat_step, lat_count), lax.rem(lon_me + lon_step, lon_count))
    return lambda: pl.semaphore_wait(barrier, lat_count - 1 + lon_count - 1 + 4)


def spectral_pass(
    lat_count,
    lon_count,
    adjoint,
    started,
    data_ref,
    first_ref,
    down_ref,
    up_ref,
    last_ref,
    mix_ref,
    padded_ref,
    part_out,
    pair_in,
    pair_out,
    cross_in,
    rows_out,
    rows_in,
    deg_out,
    deg_in,
    mixed_out,
    mixed_in,
    zonal_out,
    zonal_in,
    grid_out,
    grid_in,
    blended,
    pair_sems,
    cross_sems,
    lat_sems,
    gather_sems,
    relay_sems,
    halo_sems,
):
    row_count, lon_dev, channels = data_ref.shape
    order_share = down_ref.shape[0]
    degree_dev = mix_ref.shape[0]
    wide = 2 * channels
    share = lat_count * order_share
    modes = 2 * share
    chips = lon_count // 2
    rows_each = row_count // CHUNKS
    degrees_each = degree_dev // CHUNKS
    lat_me = lax.axis_index("lat")
    lon_me = lax.axis_index("lon")
    chip = lon_me // 2
    core = lax.rem(lon_me, 2)
    mate = 2 * chip + 1 - core
    lat_peers = [lax.rem(lat_me + step, lat_count) for step in range(1, lat_count)]
    chip_peers = [lax.rem(chip + step, chips) for step in range(1, chips)]
    lat_next = lax.rem(lat_me + 1, lat_count)
    lat_last = lax.rem(lat_me + lat_count - 1, lat_count)
    lon_next = lax.rem(lon_me + 1, lon_count)
    lon_last = lax.rem(lon_me + lon_count - 1, lon_count)
    halo_rows = {
        0: (lat_me, slice(0, row_count), slice(HW, HW + row_count)),
        1: (lat_next, slice(row_count - HW, row_count), slice(0, HW)),
        2: (lat_last, slice(0, HW), slice(HW + row_count, 2 * HW + row_count)),
    }
    halo_columns = {
        0: (lon_me, slice(0, lon_dev), slice(EDGE, EDGE + lon_dev)),
        1: (lon_next, slice(lon_dev - EDGE, lon_dev), slice(0, EDGE)),
        2: (lon_last, slice(0, EDGE), slice(EDGE + lon_dev, 2 * EDGE + lon_dev)),
    }

    def copying(source, target, sems, place, came, device):
        return pltpu.make_async_remote_copy(
            src_ref=source,
            dst_ref=target,
            send_sem=sems.at[(0,) + place],
            recv_sem=sems.at[(1,) + came],
            device_id=device,
            device_id_type=pl.DeviceIdType.MESH,
        )

    def push(source, target, sems, place, came, device):
        copy = copying(source, target, sems, place, came, device)
        copy.start()
        started.append(copy)

    def arrived(target, sems, came):
        copying(target, target, sems, came, came, (lat_me, mate)).wait_recv()

    def rows_of(number):
        return pl.ds(number * rows_each, rows_each)

    def transform(number):
        group = 8

        def body(index, carry):
            for step in range(group):
                row = number * rows_each + index * group + step
                part = jnp.dot(
                    first_ref[...], data_ref[row], preferred_element_type=jnp.float32
                ).astype(jnp.bfloat16)
                for other in range(chips):
                    for side in range(2):
                        begin = (2 * other + side) * modes
                        part_out[side, other, row] = part[begin : begin + modes]
            return carry

        lax.fori_loop(0, rows_each // group, body, 0)

    def lat_push(number, piece, source, target):
        for peer in lat_peers:
            push(
                source(peer),
                target(lat_me),
                lat_sems,
                (number, piece, peer),
                (number, piece, lat_me),
                (peer, lon_me),
            )

    def lat_arrived(number, piece, target):
        for peer in lat_peers:
            arrived(target(peer), lat_sems, (number, piece, peer))

    def begin(number):
        transform(number)

    def send(number):
        push(
            part_out.at[1 - core, :, rows_of(number)],
            pair_in.at[:, rows_of(number)],
            pair_sems,
            (number,),
            (number,),
            (lat_me, mate),
        )

    def halos_arrived():
        for r, (_, _, to_rows) in halo_rows.items():
            for c, (_, _, to_columns) in halo_columns.items():
                if r or c:
                    arrived(padded_ref.at[to_rows, to_columns], halo_sems, (3 * r + c,))

    def run(fill, finish, follow):
        for r, (lat, from_rows, to_rows) in halo_rows.items():
            for c, (lon, from_columns, to_columns) in halo_columns.items():
                if r or c:
                    push(
                        data_ref.at[from_rows, from_columns],
                        padded_ref.at[to_rows, to_columns],
                        halo_sems,
                        (3 * r + c,),
                        (3 * r + c,),
                        (lat, lon),
                    )
        for number in range(CHUNKS):
            piece = rows_of(number)
            arrived(pair_in.at[:, piece], pair_sems, (number,))
            for other in chip_peers:
                pair_out[other, piece] = (
                    part_out[core, other, piece].astype(jnp.float32)
                    + pair_in[other, piece].astype(jnp.float32)
                ).astype(jnp.bfloat16)
                push(
                    pair_out.at[other, piece],
                    cross_in.at[chip, piece],
                    cross_sems,
                    (number, other),
                    (number, chip),
                    (lat_me, 2 * other + core),
                )
        padded_ref[HW : HW + row_count, EDGE : EDGE + lon_dev] = data_ref[...]
        fill(0)
        for number in range(CHUNKS):
            piece = rows_of(number)
            total = part_out[core, chip, piece].astype(jnp.float32) + pair_in[chip, piece].astype(
                jnp.float32
            )
            for other in chip_peers:
                arrived(cross_in.at[other, piece], cross_sems, (number, other))
                total = total + cross_in[other, piece].astype(jnp.float32)
            begin = number * rows_each
            rows_out[:, :, :, begin : begin + rows_each] = (
                jnp.swapaxes(total, 0, 1)
                .astype(jnp.bfloat16)
                .reshape(lat_count, order_share, 2, rows_each, channels)
            )
            lat_push(
                0,
                number,
                lambda peer: rows_out.at[peer, :, :, piece],
                lambda peer: rows_in.at[peer, :, :, piece],
            )
        rows_in[lat_me] = rows_out[lat_me]
        fill(1)
        for number in range(CHUNKS):
            piece = rows_of(number)
            lat_arrived(0, number, lambda peer: rows_in.at[peer, :, :, piece])

        for e in range(order_share):
            columns = jnp.concatenate(
                [rows_in[:, e, part].reshape(lat_count * row_count, channels) for part in range(2)],
                axis=1,
            )
            degrees = jnp.dot(down_ref[e], columns, preferred_element_type=jnp.float32)
            deg_out[:, e] = degrees.astype(jnp.bfloat16).reshape(lat_count, degree_dev, wide)
        for number in range(CHUNKS):
            piece = pl.ds(number * degrees_each, degrees_each)
            lat_push(
                1,
                number,
                lambda peer: deg_out.at[peer, :, piece],
                lambda peer: deg_in.at[peer, :, piece],
            )
        deg_in[lat_me] = deg_out[lat_me]
        fill(2)

        for number in range(CHUNKS):
            begin = number * degrees_each
            piece = pl.ds(begin, degrees_each)
            lat_arrived(1, number, lambda peer: deg_in.at[peer, :, piece])
            by_degree = deg_in[:, :, begin : begin + degrees_each].reshape(share, degrees_each, wide)
            turned = jnp.swapaxes(by_degree.astype(jnp.float32), 0, 1).astype(jnp.bfloat16)
            for step in range(degrees_each):
                degree = begin + step
                pair = jnp.concatenate([turned[step, :, :channels], turned[step, :, channels:]], axis=0)
                if adjoint:
                    weights = jnp.concatenate([mix_ref[degree, 0], mix_ref[degree, 1]], axis=0)
                    product = lax.dot_general(
                        pair, weights, (((1,), (1,)), ((), ())), preferred_element_type=jnp.float32
                    )
                else:
                    weights = jnp.concatenate([mix_ref[degree, 0], mix_ref[degree, 1]], axis=1)
                    product = jnp.dot(pair, weights, preferred_element_type=jnp.float32)
                sign = -1.0 if adjoint else 1.0
                blended[step, :, :channels] = (
                    product[:share, :channels] - sign * product[share:, channels:]
                )
                blended[step, :, channels:] = (
                    sign * product[:share, channels:] + product[share:, :channels]
                )
            mixed_out[:, :, begin : begin + degrees_each] = (
                jnp.swapaxes(blended[...], 0, 1)
                .astype(jnp.bfloat16)
                .reshape(lat_count, order_share, degrees_each, wide)
            )
            lat_push(
                2,
                number,
                lambda peer: mixed_out.at[peer, :, piece],
                lambda peer: mixed_in.at[peer, :, piece],
            )
        mixed_in[lat_me] = mixed_out[lat_me]
        fill(3)
        for number in range(CHUNKS):
            piece = pl.ds(number * degrees_each, degrees_each)
            lat_arrived(2, number, lambda peer: mixed_in.at[peer, :, piece])

        for e in range(order_share):
            spectrum = mixed_in[:, e].reshape(lat_count * degree_dev, wide)
            zonal = lax.dot_general(
                up_ref[e], spectrum, (((0,), (0,)), ((), ())), preferred_element_type=jnp.float32
            ).astype(jnp.bfloat16)
            for part in range(2):
                zonal_out[:, e, part] = zonal[:, part * channels : (part + 1) * channels].reshape(
                    lat_count, row_count, channels
                )
        for number in range(CHUNKS):
            piece = rows_of(number)
            lat_push(
                3,
                number,
                lambda peer: zonal_out.at[peer, :, :, piece],
                lambda peer: zonal_in.at[peer, :, :, piece],
            )
        zonal_in[lat_me] = zonal_out[lat_me]
        fill(4)

        for number in range(CHUNKS):
            piece = rows_of(number)
            begin = number * rows_each
            lat_arrived(3, number, lambda peer: zonal_in.at[peer, :, :, piece])
            by_order = zonal_in[:, :, :, begin : begin + rows_each].reshape(modes, rows_each, channels)
            grid_out[piece] = jnp.swapaxes(by_order.astype(jnp.float32), 0, 1).astype(jnp.bfloat16)
            for lon in [2 * other + core for other in chip_peers] + [mate]:
                push(
                    grid_out.at[piece],
                    grid_in.at[lon_me, piece],
                    gather_sems,
                    (number, lon),
                    (number, lon_me),
                    (lat_me, lon),
                )
            grid_in[lon_me, piece] = grid_out[piece]
        fill(5)
        for number in range(CHUNKS):
            piece = rows_of(number)
            for other in chip_peers:
                slot = 2 * other + core
                arrived(grid_in.at[slot, piece], gather_sems, (number, slot))
                push(
                    grid_in.at[slot, piece],
                    grid_in.at[slot, piece],
                    relay_sems,
                    (number, slot),
                    (number, slot),
                    (lat_me, mate),
                )
        for number in range(CHUNKS):
            piece = rows_of(number)
            arrived(grid_in.at[mate, piece], gather_sems, (number, mate))
            for other in chip_peers:
                slot = 2 * other + 1 - core
                arrived(grid_in.at[slot, piece], relay_sems, (number, slot))

            def restore(index, carry):
                for step in range(8):
                    row = number * rows_each + index * 8 + step
                    every = grid_in[:, row].reshape(lon_count * modes, channels)
                    finish(
                        row,
                        jnp.dot(last_ref[...], every, preferred_element_type=jnp.float32)
                        .astype(jnp.bfloat16)
                        .astype(jnp.float32),
                    )
                return carry

            lax.fori_loop(0, rows_each // 8, restore, 0)
            follow(number)


    return begin, send, run, halos_arrived


def toeplitz(taps, count):
    spread = [
        pltpu.roll(
            jnp.broadcast_to(taps[k : k + 1, :], (count, taps.shape[1])),
            0,
            1,
            stride=1,
            stride_axis=0,
        )
        for k in range(taps.shape[0])
    ]
    return jnp.concatenate(spread, axis=0).astype(jnp.bfloat16)


def stretch(padded_ref, whole_ref):
    width = whole_ref.shape[1]

    def body(row, carry):
        whole_ref[row] = padded_ref[row].astype(jnp.float32)[HW : HW + width]
        return carry

    lax.fori_loop(0, whole_ref.shape[0], body, 0)


def whole_kernel(
    lat_count,
    lon_count,
    gain_ref,
    back_ref,
    orders_ref,
    sources_ref,
    near_ref,
    trig_ref,
    fields_ref,
    to_rows_ref,
    to_ref,
    from_rows_ref,
    from_ref,
    taps_ref,
    back_taps_ref,
    weight_ref,
    turned_weight_ref,
    cotangent_any,
    mix_any,
    out_ref,
    grad_ref,
    weighted,
    plain,
    mix,
    cotangent,
    padded,
    grad_padded,
    whole,
    conv,
    grad_mix,
    pieces,
    load_sems,
    *scratch,
):
    row_count, lon_dev, channels = fields_ref.shape
    tall, width, _ = whole.shape
    kernel_count = taps_ref.shape[1]
    band_count = sources_ref.shape[1]
    lanes = taps_ref.shape[2]
    wait_entry = enter(lat_count, lon_count)
    mix_load = pltpu.make_async_copy(mix_any, mix, load_sems.at[0])
    cotangent_load = pltpu.make_async_copy(cotangent_any, cotangent, load_sems.at[1])
    mix_load.start()
    cotangent_load.start()
    started = []
    half = len(scratch) // 2
    begin, send, run, halos = spectral_pass(
        lat_count,
        lon_count,
        False,
        started,
        fields_ref,
        to_rows_ref,
        weighted,
        plain,
        from_ref,
        mix,
        padded,
        *scratch[:half],
    )
    begin_back, send_back, run_back, halos_back = spectral_pass(
        lat_count,
        lon_count,
        True,
        started,
        grad_mix,
        from_rows_ref,
        plain,
        weighted,
        to_ref,
        mix,
        grad_padded,
        *scratch[half:],
    )

    def local_rows(first):
        def one(row):
            spare = jnp.zeros((lanes - band_count * width, channels), jnp.float32)
            sources = jnp.concatenate(
                [whole[sources_ref[row, band]] for band in range(band_count)] + [spare], axis=0
            ).astype(jnp.bfloat16)
            terms = jnp.dot(
                toeplitz(taps_ref[row], lon_dev), sources, preferred_element_type=jnp.float32
            ).astype(jnp.bfloat16)
            flat = jnp.concatenate(
                [terms[k * lon_dev : (k + 1) * lon_dev] for k in range(kernel_count)], axis=1
            )
            conv[row] = jnp.dot(flat, weight_ref[...], preferred_element_type=jnp.float32)

        def body(index, carry):
            for step in range(4):
                one(first + 4 * index + step)
            return carry

        lax.fori_loop(0, row_count // 16, body, 0)

    def fill(point):
        if point == 0:
            legendre_kernel(gain_ref, back_ref, orders_ref, trig_ref, weighted, plain)
        if point == 1:
            halos()
            stretch(padded, whole)
        if point == 2:
            mix_load.wait()
        if 1 <= point <= 4:
            local_rows((point - 1) * (row_count // 4))

    def finish(row, spectral):
        activation, derivative = gelu_parts(spectral + conv[row])
        out_ref[row] = (fields_ref[row].astype(jnp.float32) + activation).astype(jnp.bfloat16)
        grad_mix[row] = (cotangent[row].astype(jnp.float32) * derivative).astype(jnp.bfloat16)

    def follow(number):
        begin_back(number)
        send_back(number)

    for number in range(CHUNKS):
        begin(number)
        if number == 0:
            wait_entry()
        send(number)
    cotangent_load.wait()
    run(fill, finish, follow)

    def adjoint_rows(first):
        def one(row):
            spare = jnp.zeros((lanes - kernel_count * width, channels), jnp.bfloat16)
            grads = jnp.dot(
                whole[row].astype(jnp.bfloat16),
                turned_weight_ref[...],
                preferred_element_type=jnp.float32,
            ).astype(jnp.bfloat16)
            stacked = jnp.concatenate(
                [grads[:, k * channels : (k + 1) * channels] for k in range(kernel_count)] + [spare],
                axis=0,
            )
            spread = jnp.dot(
                toeplitz(back_taps_ref[row], lon_dev), stacked, preferred_element_type=jnp.float32
            )
            for band in range(band_count):
                pieces[row, band] = spread[band * lon_dev : (band + 1) * lon_dev]

        def body(index, carry):
            for step in range(4):
                one(first + 4 * index + step)
            return carry

        lax.fori_loop(0, tall // 16, body, 0)

    def gathered(row, full_first, full_last):
        total = cotangent[row].astype(jnp.float32)
        for band in range(band_count):
            offsets = range(2 * HW + 1)
            if band == 0 and not full_first:
                offsets = [2 * HW]
            if band == band_count - 1 and not full_last:
                offsets = [0]
            for offset in offsets:
                hit = near_ref[row + offset, band] == row
                total = total + jnp.where(hit, 1.0, 0.0) * pieces[row + offset, band]
        conv[row] = total

    def fill_back(point):
        if point == 1:
            halos_back()
            stretch(grad_padded, whole)
        if 1 <= point <= 4:
            adjoint_rows((point - 1) * (tall // 4))
        if point == 5:
            gathered(0, True, False)
            gathered(row_count - 1, False, True)

            def body(row, carry):
                gathered(row, False, False)
                return carry

            lax.fori_loop(1, row_count - 1, body, 0)

    def finish_back(row, spectral):
        grad_ref[row] = (conv[row] + spectral).astype(jnp.bfloat16)

    run_back(fill_back, finish_back, lambda number: None)
    for copy in started:
        copy.wait_send()


def pass_scratch(lat_count, lon_count, row_count, order_share, degree_dev, channels):
    share = lat_count * order_share
    wide = 2 * channels
    chips = lon_count // 2
    bf16 = jnp.bfloat16
    part = pltpu.VMEM((chips, row_count, 2 * share, channels), bf16)
    rows = pltpu.VMEM((lat_count, order_share, 2, row_count, channels), bf16)
    degrees = pltpu.VMEM((lat_count, order_share, degree_dev, wide), bf16)
    return [
        pltpu.VMEM((2, chips, row_count, 2 * share, channels), bf16),
        part,
        part,
        part,
        rows,
        rows,
        degrees,
        degrees,
        degrees,
        degrees,
        rows,
        rows,
        pltpu.VMEM((row_count, 2 * share, channels), bf16),
        pltpu.VMEM((lon_count, row_count, 2 * share, channels), bf16),
        pltpu.VMEM((degree_dev // CHUNKS, share, wide), jnp.float32),
        pltpu.SemaphoreType.DMA((2, CHUNKS)),
        pltpu.SemaphoreType.DMA((2, CHUNKS, chips)),
        pltpu.SemaphoreType.DMA((2, 4, CHUNKS, lat_count)),
        pltpu.SemaphoreType.DMA((2, CHUNKS, lon_count)),
        pltpu.SemaphoreType.DMA((2, CHUNKS, lon_count)),
        pltpu.SemaphoreType.DMA((2, 9)),
    ]


def tap_rows(basis, width):
    flat = jnp.pad(basis, ((0, 0), (0, 0), (0, 0), (0, width - basis.shape[3])))
    flat = flat.reshape(basis.shape[0], basis.shape[1], basis.shape[2] * width)
    lanes = -(-flat.shape[2] // 128) * 128
    return jnp.pad(flat, ((0, 0), (0, 0), (0, lanes - flat.shape[2]))).astype(jnp.float32)


def per_device(fields, cotangent, spectral_weight, local_weight, filter_basis, neighbor_rows):
    lat_count = lax.axis_size("lat")
    lon_count = lax.axis_size("lon")
    lat_index = lax.axis_index("lat")
    lon_index = lax.axis_index("lon")
    _, lat_dev, lon_dev, channels = fields.shape
    degree_dev = spectral_weight.shape[0]
    kernel_count = filter_basis.shape[0]
    total_lat = lat_dev * lat_count
    total_lon = lon_dev * lon_count
    order_share = MDEV // lat_count
    width = lon_dev + 2 * HW
    tall = lat_dev + 2 * HW
    to_modes, from_modes = mode_tables(total_lon, MDEV * lon_count)
    table_shape = (lon_dev, 2, lon_count, lat_count, order_share)
    to_modes = lax.dynamic_slice_in_dim(to_modes, lon_index * lon_dev, lon_dev, 0)
    from_modes = lax.dynamic_slice_in_dim(from_modes, lon_index * lon_dev, lon_dev, 0)
    to_modes = to_modes.reshape(table_shape).transpose(0, 2, 3, 4, 1).reshape(lon_dev, -1)
    from_modes = from_modes.reshape(table_shape).transpose(0, 2, 3, 4, 1).reshape(lon_dev, -1)
    orders = (
        lon_index * MDEV + lat_index * order_share + jnp.arange(order_share, dtype=jnp.int32)
    )
    gain, back_gain, trig = legendre_inputs(orders, degree_dev * lat_count, total_lat)
    row_base = lat_index * lat_dev
    near_rows = lax.dynamic_slice_in_dim(
        jnp.pad(neighbor_rows, ((HW, HW), (0, 0))), row_base, tall, 0
    )
    near_basis = lax.dynamic_slice_in_dim(
        jnp.pad(filter_basis, ((0, 0), (HW, HW), (0, 0), (0, 0))), row_base, tall, 1
    )
    sources = near_rows[HW : HW + lat_dev] - row_base + HW
    taps = tap_rows(near_basis[:, HW : HW + lat_dev].transpose(1, 0, 2, 3), width)
    back_taps = tap_rows(near_basis[..., ::-1].transpose(1, 2, 0, 3), width)
    smem = pl.BlockSpec(memory_space=pltpu.SMEM)
    vmem = pl.BlockSpec(memory_space=pltpu.VMEM)
    grid = jax.ShapeDtypeStruct((lat_dev, lon_dev, channels), jnp.bfloat16)
    bf16 = jnp.bfloat16
    table = pltpu.VMEM((order_share, degree_dev * lat_count, total_lat), bf16)
    rim = pltpu.VMEM((tall, lon_dev + 2 * EDGE, channels), bf16)
    passes = pass_scratch(lat_count, lon_count, lat_dev, order_share, degree_dev, channels)
    block_output, input_grad = pl.pallas_call(
        functools.partial(whole_kernel, lat_count, lon_count),
        out_shape=(grid, grid),
        in_specs=[smem] * 5 + [vmem] * 10 + [pl.BlockSpec(memory_space=pl.ANY)] * 2,
        out_specs=(vmem, vmem),
        scratch_shapes=[
            table,
            table,
            pltpu.VMEM(spectral_weight.shape, bf16),
            pltpu.VMEM((lat_dev, lon_dev, channels), bf16),
            rim,
            rim,
            pltpu.VMEM((tall, width, channels), jnp.float32),
            pltpu.VMEM((lat_dev, lon_dev, channels), jnp.float32),
            pltpu.VMEM((lat_dev, lon_dev, channels), bf16),
            pltpu.VMEM((tall, filter_basis.shape[2], lon_dev, channels), jnp.float32),
            pltpu.SemaphoreType.DMA((2,)),
        ]
        + passes
        + passes,
        compiler_params=pltpu.CompilerParams(
            collective_id=0, has_side_effects=True, vmem_limit_bytes=56 * 1024 * 1024
        ),
        name="operator_block",
    )(
        gain,
        back_gain,
        orders,
        sources,
        near_rows - row_base,
        trig,
        fields[0],
        to_modes.T,
        to_modes,
        from_modes.T,
        from_modes,
        taps,
        back_taps,
        local_weight.reshape(-1, channels),
        local_weight.transpose(2, 0, 1).reshape(channels, kernel_count * channels),
        cotangent[0],
        spectral_weight,
    )
    return (block_output[None], input_grad[None])


def solution(mesh):
    in_specs = (
        P(None, "lat", "lon", None),
        P(None, "lat", "lon", None),
        P("lat", None, None, None),
        P(),
        P(),
        P(),
    )
    out_specs = (P(None, "lat", "lon", None), P(None, "lat", "lon", None))
    return jax.shard_map(
        per_device, mesh=mesh, in_specs=in_specs, out_specs=out_specs, check_vma=False
    )
```

```python
import functools
import math

import jax
import jax.numpy as jnp
from jax import lax
from jax.experimental import pallas as pl
from jax.experimental.pallas import tpu as pltpu
from jax.sharding import PartitionSpec as P

MDEV = 16
HW = 8


TANH_SCALE = 0.7978845608028654
CUBIC_TERM = 0.044715


def gelu_parts(values):
    tanh_input = TANH_SCALE * (values + CUBIC_TERM * values * values * values)
    hyper = jnp.tanh(tanh_input)
    result = 0.5 * values * (1.0 + hyper)
    derivative = 0.5 * (1.0 + hyper) + 0.5 * values * (1.0 - hyper * hyper) * TANH_SCALE * (
        1.0 + 3.0 * CUBIC_TERM * values * values
    )
    return (result, derivative)


def mode_tables(lon_count, mode_count):
    angles_int = (
        jnp.arange(lon_count, dtype=jnp.int32)[:, None]
        * jnp.arange(mode_count, dtype=jnp.int32)[None, :]
        % lon_count
    )
    angles = angles_int.astype(jnp.float32) * (2.0 * math.pi / lon_count)
    stacked = jnp.stack([jnp.cos(angles), -jnp.sin(angles)], axis=1)
    orders = jnp.arange(mode_count, dtype=jnp.int32)
    factor = jnp.where(orders == 0, 1.0, 2.0).astype(jnp.float32)
    to_modes = (stacked * (2.0 * math.pi / lon_count)).astype(jnp.bfloat16)
    from_modes = (stacked * factor[None, None, :]).astype(jnp.bfloat16)
    return (to_modes, from_modes)


STEP = 16


def legendre_kernel(gain_ref, back_ref, orders_ref, trig_ref, weighted_ref, plain_ref):
    order_share, degree_count, _ = plain_ref.shape
    cosine = trig_ref[0:1, :]
    quadrature = trig_ref[1:2, :]

    def block(index, state):
        carried = []
        for e in range(order_share):
            value, previous, log_scale = state[3 * e : 3 * e + 3]
            order = orders_ref[e]
            rows = []
            for step in range(STEP):
                degree = index * STEP + step
                active = degree > order
                following = gain_ref[e, degree] * (cosine * value) - back_ref[e, degree] * previous
                previous = jnp.where(active, value, previous)
                value = jnp.where(active, following, value)
                rows.append(jnp.where(degree >= order, value, 0.0))
            stacked = jnp.concatenate(rows, axis=0) * jnp.exp(log_scale)
            place = pl.ds(pl.multiple_of(index * STEP, STEP), STEP)
            plain_ref[e, place, :] = stacked.astype(jnp.bfloat16)
            weighted_ref[e, place, :] = (stacked * quadrature).astype(jnp.bfloat16)
            largest = jnp.maximum(jnp.abs(value), jnp.abs(previous))
            carried += [value / largest, previous / largest, log_scale + jnp.log(largest)]
        return tuple(carried)

    start = []
    for e in range(order_share):
        seed = trig_ref[2 + e : 3 + e, :]
        start += [jnp.ones_like(seed), jnp.zeros_like(seed), seed]
    lax.fori_loop(0, degree_count // STEP, block, tuple(start))


def legendre_inputs(orders, degree_count, lat_count):
    order_share = orders.shape[0]
    colatitude = math.pi * (jnp.arange(lat_count, dtype=jnp.float32) + 0.5) / lat_count
    sine_part = jnp.sin(colatitude)
    order_real = orders.astype(jnp.float32)
    seed_log = 0.5 * (
        jnp.log((2.0 * order_real + 1.0) / (4.0 * math.pi))
        + lax.lgamma(order_real + 0.5)
        - lax.lgamma(order_real + 1.0)
        - 0.5 * math.log(math.pi)
    )
    seed_log = seed_log[:, None] + order_real[:, None] * jnp.log(sine_part)[None, :]
    degree_real = jnp.arange(degree_count, dtype=jnp.float32)[None, :]
    order_row = order_real[:, None]
    forward_gain = jnp.sqrt(
        jnp.maximum(4.0 * degree_real * degree_real - 1.0, 1.0)
        / jnp.maximum(degree_real * degree_real - order_row * order_row, 1.0)
    )
    backward_gain = jnp.sqrt(
        jnp.maximum((degree_real - 1.0) ** 2 - order_row * order_row, 0.0)
        / jnp.maximum(4.0 * (degree_real - 1.0) ** 2 - 1.0, 1.0)
    )
    trig = jnp.concatenate(
        [
            jnp.cos(colatitude)[None, :],
            (math.pi / lat_count * sine_part)[None, :],
            seed_log,
        ],
        axis=0,
    )
    return (forward_gain, forward_gain * backward_gain, trig)


CHUNKS = 2
EDGE = 2 * HW


def place_of(lat_count, lon_count):
    lat_me = lax.axis_index("lat")
    lon_me = lax.axis_index("lon")
    return lat_me, lon_me


def enter(lat_count, lon_count):
    lat_me, lon_me = place_of(lat_count, lon_count)
    barrier = pltpu.get_barrier_semaphore()

    def greet(lat, lon):
        pl.semaphore_signal(
            barrier, inc=1, device_id=(lat, lon), device_id_type=pl.DeviceIdType.MESH
        )

    for step in range(1, lat_count):
        greet(lax.rem(lat_me + step, lat_count), lon_me)
    for step in range(1, lon_count):
        greet(lat_me, lax.rem(lon_me + step, lon_count))
    for lat_step in (1, lat_count - 1):
        for lon_step in (1, lon_count - 1):
            greet(lax.rem(lat_me + lat_step, lat_count), lax.rem(lon_me + lon_step, lon_count))
    return lambda: pl.semaphore_wait(barrier, lat_count - 1 + lon_count - 1 + 4)


def spectral_pass(
    lat_count,
    lon_count,
    adjoint,
    started,
    data_ref,
    first_ref,
    down_ref,
    up_ref,
    last_ref,
    mix_ref,
    padded_ref,
    part_out,
    pair_in,
    pair_out,
    cross_in,
    rows_out,
    rows_in,
    deg_out,
    deg_in,
    mixed_out,
    mixed_in,
    zonal_out,
    zonal_in,
    grid_out,
    grid_in,
    blended,
    pair_sems,
    cross_sems,
    lat_sems,
    gather_sems,
    relay_sems,
    halo_sems,
):
    row_count, lon_dev, channels = data_ref.shape
    order_share = down_ref.shape[0]
    degree_dev = mix_ref.shape[0]
    wide = 2 * channels
    share = lat_count * order_share
    modes = 2 * share
    chips = lon_count // 2
    rows_each = row_count // CHUNKS
    degrees_each = degree_dev // CHUNKS
    lat_me = lax.axis_index("lat")
    lon_me = lax.axis_index("lon")
    chip = lon_me // 2
    core = lax.rem(lon_me, 2)
    mate = 2 * chip + 1 - core
    lat_peers = [lax.rem(lat_me + step, lat_count) for step in range(1, lat_count)]
    chip_peers = [lax.rem(chip + step, chips) for step in range(1, chips)]
    lat_next = lax.rem(lat_me + 1, lat_count)
    lat_last = lax.rem(lat_me + lat_count - 1, lat_count)
    lon_next = lax.rem(lon_me + 1, lon_count)
    lon_last = lax.rem(lon_me + lon_count - 1, lon_count)
    halo_rows = {
        0: (lat_me, slice(0, row_count), slice(HW, HW + row_count)),
        1: (lat_next, slice(row_count - HW, row_count), slice(0, HW)),
        2: (lat_last, slice(0, HW), slice(HW + row_count, 2 * HW + row_count)),
    }
    halo_columns = {
        0: (lon_me, slice(0, lon_dev), slice(EDGE, EDGE + lon_dev)),
        1: (lon_next, slice(lon_dev - EDGE, lon_dev), slice(0, EDGE)),
        2: (lon_last, slice(0, EDGE), slice(EDGE + lon_dev, 2 * EDGE + lon_dev)),
    }

    def copying(source, target, sems, place, came, device):
        return pltpu.make_async_remote_copy(
            src_ref=source,
            dst_ref=target,
            send_sem=sems.at[(0,) + place],
            recv_sem=sems.at[(1,) + came],
            device_id=device,
            device_id_type=pl.DeviceIdType.MESH,
        )

    def push(source, target, sems, place, came, device):
        copy = copying(source, target, sems, place, came, device)
        copy.start()
        started.append(copy)

    def arrived(target, sems, came):
        copying(target, target, sems, came, came, (lat_me, mate)).wait_recv()

    def rows_of(number):
        return pl.ds(number * rows_each, rows_each)

    def transform(number):
        group = 8

        def body(index, carry):
            for step in range(group):
                row = number * rows_each + index * group + step
                part = jnp.dot(
                    first_ref[...], data_ref[row], preferred_element_type=jnp.float32
                ).astype(jnp.bfloat16)
                for other in range(chips):
                    for side in range(2):
                        begin = (2 * other + side) * modes
                        part_out[side, other, row] = part[begin : begin + modes]
            return carry

        lax.fori_loop(0, rows_each // group, body, 0)

    def lat_push(number, piece, source, target):
        for peer in lat_peers:
            push(
                source(peer),
                target(lat_me),
                lat_sems,
                (number, piece, peer),
                (number, piece, lat_me),
                (peer, lon_me),
            )

    def lat_arrived(number, piece, target):
        for peer in lat_peers:
            arrived(target(peer), lat_sems, (number, piece, peer))

    def begin(number):
        transform(number)

    def send(number):
        push(
            part_out.at[1 - core, :, rows_of(number)],
            pair_in.at[:, rows_of(number)],
            pair_sems,
            (number,),
            (number,),
            (lat_me, mate),
        )

    def halos_arrived():
        for r, (_, _, to_rows) in halo_rows.items():
            for c, (_, _, to_columns) in halo_columns.items():
                if r or c:
                    arrived(padded_ref.at[to_rows, to_columns], halo_sems, (3 * r + c,))

    def run(fill, finish, follow):
        for r, (lat, from_rows, to_rows) in halo_rows.items():
            for c, (lon, from_columns, to_columns) in halo_columns.items():
                if r or c:
                    push(
                        data_ref.at[from_rows, from_columns],
                        padded_ref.at[to_rows, to_columns],
                        halo_sems,
                        (3 * r + c,),
                        (3 * r + c,),
                        (lat, lon),
                    )
        for number in range(CHUNKS):
            piece = rows_of(number)
            arrived(pair_in.at[:, piece], pair_sems, (number,))
            for other in chip_peers:
                pair_out[other, piece] = (
                    part_out[core, other, piece].astype(jnp.float32)
                    + pair_in[other, piece].astype(jnp.float32)
                ).astype(jnp.bfloat16)
                push(
                    pair_out.at[other, piece],
                    cross_in.at[chip, piece],
                    cross_sems,
                    (number, other),
                    (number, chip),
                    (lat_me, 2 * other + core),
                )
        padded_ref[HW : HW + row_count, EDGE : EDGE + lon_dev] = data_ref[...]
        fill(0)
        for number in range(CHUNKS):
            piece = rows_of(number)
            total = part_out[core, chip, piece].astype(jnp.float32) + pair_in[chip, piece].astype(
                jnp.float32
            )
            for other in chip_peers:
                arrived(cross_in.at[other, piece], cross_sems, (number, other))
                total = total + cross_in[other, piece].astype(jnp.float32)
            begin = number * rows_each
            rows_out[:, :, :, begin : begin + rows_each] = (
                jnp.swapaxes(total, 0, 1)
                .astype(jnp.bfloat16)
                .reshape(lat_count, order_share, 2, rows_each, channels)
            )
            lat_push(
                0,
                number,
                lambda peer: rows_out.at[peer, :, :, piece],
                lambda peer: rows_in.at[peer, :, :, piece],
            )
        rows_in[lat_me] = rows_out[lat_me]
        fill(1)
        for number in range(CHUNKS):
            piece = rows_of(number)
            lat_arrived(0, number, lambda peer: rows_in.at[peer, :, :, piece])

        for e in range(order_share):
            columns = jnp.concatenate(
                [rows_in[:, e, part].reshape(lat_count * row_count, channels) for part in range(2)],
                axis=1,
            )
            degrees = jnp.dot(down_ref[e], columns, preferred_element_type=jnp.float32)
            deg_out[:, e] = degrees.astype(jnp.bfloat16).reshape(lat_count, degree_dev, wide)
        for number in range(CHUNKS):
            piece = pl.ds(number * degrees_each, degrees_each)
            lat_push(
                1,
                number,
                lambda peer: deg_out.at[peer, :, piece],
                lambda peer: deg_in.at[peer, :, piece],
            )
        deg_in[lat_me] = deg_out[lat_me]
        fill(2)

        for number in range(CHUNKS):
            begin = number * degrees_each
            piece = pl.ds(begin, degrees_each)
            lat_arrived(1, number, lambda peer: deg_in.at[peer, :, piece])
            by_degree = deg_in[:, :, begin : begin + degrees_each].reshape(share, degrees_each, wide)
            turned = jnp.swapaxes(by_degree.astype(jnp.float32), 0, 1).astype(jnp.bfloat16)
            for step in range(degrees_each):
                degree = begin + step
                pair = jnp.concatenate([turned[step, :, :channels], turned[step, :, channels:]], axis=0)
                if adjoint:
                    weights = jnp.concatenate([mix_ref[degree, 0], mix_ref[degree, 1]], axis=0)
                    product = lax.dot_general(
                        pair, weights, (((1,), (1,)), ((), ())), preferred_element_type=jnp.float32
                    )
                else:
                    weights = jnp.concatenate([mix_ref[degree, 0], mix_ref[degree, 1]], axis=1)
                    product = jnp.dot(pair, weights, preferred_element_type=jnp.float32)
                sign = -1.0 if adjoint else 1.0
                blended[step, :, :channels] = (
                    product[:share, :channels] - sign * product[share:, channels:]
                )
                blended[step, :, channels:] = (
                    sign * product[:share, channels:] + product[share:, :channels]
                )
            mixed_out[:, :, begin : begin + degrees_each] = (
                jnp.swapaxes(blended[...], 0, 1)
                .astype(jnp.bfloat16)
                .reshape(lat_count, order_share, degrees_each, wide)
            )
            lat_push(
                2,
                number,
                lambda peer: mixed_out.at[peer, :, piece],
                lambda peer: mixed_in.at[peer, :, piece],
            )
        mixed_in[lat_me] = mixed_out[lat_me]
        fill(3)
        for number in range(CHUNKS):
            piece = pl.ds(number * degrees_each, degrees_each)
            lat_arrived(2, number, lambda peer: mixed_in.at[peer, :, piece])

        for e in range(order_share):
            spectrum = mixed_in[:, e].reshape(lat_count * degree_dev, wide)
            zonal = lax.dot_general(
                up_ref[e], spectrum, (((0,), (0,)), ((), ())), preferred_element_type=jnp.float32
            ).astype(jnp.bfloat16)
            for part in range(2):
                zonal_out[:, e, part] = zonal[:, part * channels : (part + 1) * channels].reshape(
                    lat_count, row_count, channels
                )
        for number in range(CHUNKS):
            piece = rows_of(number)
            lat_push(
                3,
                number,
                lambda peer: zonal_out.at[peer, :, :, piece],
                lambda peer: zonal_in.at[peer, :, :, piece],
            )
        zonal_in[lat_me] = zonal_out[lat_me]
        fill(4)

        for number in range(CHUNKS):
            piece = rows_of(number)
            begin = number * rows_each
            lat_arrived(3, number, lambda peer: zonal_in.at[peer, :, :, piece])
            by_order = zonal_in[:, :, :, begin : begin + rows_each].reshape(modes, rows_each, channels)
            grid_out[piece] = jnp.swapaxes(by_order.astype(jnp.float32), 0, 1).astype(jnp.bfloat16)
            for lon in [2 * other + core for other in chip_peers] + [mate]:
                push(
                    grid_out.at[piece],
                    grid_in.at[lon_me, piece],
                    gather_sems,
                    (number, lon),
                    (number, lon_me),
                    (lat_me, lon),
                )
            grid_in[lon_me, piece] = grid_out[piece]
        fill(5)
        for number in range(CHUNKS):
            piece = rows_of(number)
            for other in chip_peers:
                slot = 2 * other + core
                arrived(grid_in.at[slot, piece], gather_sems, (number, slot))
                push(
                    grid_in.at[slot, piece],
                    grid_in.at[slot, piece],
                    relay_sems,
                    (number, slot),
                    (number, slot),
                    (lat_me, mate),
                )
        for number in range(CHUNKS):
            piece = rows_of(number)
            arrived(grid_in.at[mate, piece], gather_sems, (number, mate))
            for other in chip_peers:
                slot = 2 * other + 1 - core
                arrived(grid_in.at[slot, piece], relay_sems, (number, slot))

            def restore(index, carry):
                for step in range(8):
                    row = number * rows_each + index * 8 + step
                    every = grid_in[:, row].reshape(lon_count * modes, channels)
                    finish(
                        row,
                        jnp.dot(last_ref[...], every, preferred_element_type=jnp.float32)
                        .astype(jnp.bfloat16)
                        .astype(jnp.float32),
                    )
                return carry

            lax.fori_loop(0, rows_each // 8, restore, 0)
            follow(number)


    return begin, send, run, halos_arrived


def toeplitz(taps, count):
    spread = [
        pltpu.roll(
            jnp.broadcast_to(taps[k : k + 1, :], (count, taps.shape[1])),
            0,
            1,
            stride=1,
            stride_axis=0,
        )
        for k in range(taps.shape[0])
    ]
    return jnp.concatenate(spread, axis=0).astype(jnp.bfloat16)


def stretch(padded_ref, whole_ref):
    width = whole_ref.shape[1]

    def body(row, carry):
        whole_ref[row] = padded_ref[row].astype(jnp.float32)[HW : HW + width]
        return carry

    lax.fori_loop(0, whole_ref.shape[0], body, 0)


def whole_kernel(
    lat_count,
    lon_count,
    gain_ref,
    back_ref,
    orders_ref,
    near_ref,
    trig_ref,
    fields_ref,
    to_rows_ref,
    from_rows_ref,
    taps_ref,
    back_taps_ref,
    weight_ref,
    cotangent_any,
    mix_any,
    out_ref,
    grad_ref,
    weighted,
    plain,
    mix,
    cotangent,
    padded,
    grad_padded,
    whole,
    conv,
    grad_mix,
    pieces,
    to_ref,
    from_ref,
    load_sems,
    *scratch,
):
    row_count, lon_dev, channels = fields_ref.shape
    tall, width, _ = whole.shape
    kernel_count = taps_ref.shape[1]
    band_count = near_ref.shape[1]
    lanes = taps_ref.shape[2]
    wait_entry = enter(lat_count, lon_count)
    mix_load = pltpu.make_async_copy(mix_any, mix, load_sems.at[0])
    cotangent_load = pltpu.make_async_copy(cotangent_any, cotangent, load_sems.at[1])
    mix_load.start()
    cotangent_load.start()
    started = []
    half = len(scratch) // 2
    begin, send, run, halos = spectral_pass(
        lat_count,
        lon_count,
        False,
        started,
        fields_ref,
        to_rows_ref,
        weighted,
        plain,
        from_ref,
        mix,
        padded,
        *scratch[:half],
    )
    begin_back, send_back, run_back, halos_back = spectral_pass(
        lat_count,
        lon_count,
        True,
        started,
        grad_mix,
        from_rows_ref,
        plain,
        weighted,
        to_ref,
        mix,
        grad_padded,
        *scratch[half:],
    )

    def local_rows(first):
        def one(row):
            spare = jnp.zeros((lanes - band_count * width, channels), jnp.float32)
            sources = jnp.concatenate(
                [whole[near_ref[row + HW, band] + HW] for band in range(band_count)] + [spare], axis=0
            ).astype(jnp.bfloat16)
            terms = jnp.dot(
                toeplitz(taps_ref[row], lon_dev), sources, preferred_element_type=jnp.float32
            ).astype(jnp.bfloat16)
            flat = jnp.concatenate(
                [terms[k * lon_dev : (k + 1) * lon_dev] for k in range(kernel_count)], axis=1
            )
            conv[row] = jnp.dot(flat, weight_ref[...], preferred_element_type=jnp.float32)

        def body(index, carry):
            for step in range(4):
                one(first + 4 * index + step)
            return carry

        lax.fori_loop(0, row_count // 16, body, 0)

    def fill(point):
        if point == 0:
            for rows_ref, columns_ref in ((to_rows_ref, to_ref), (from_rows_ref, from_ref)):
                columns_ref[...] = rows_ref[...].astype(jnp.float32).T.astype(jnp.bfloat16)
        if point == 1:
            legendre_kernel(gain_ref, back_ref, orders_ref, trig_ref, weighted, plain)
            halos()
            stretch(padded, whole)
        if point == 2:
            mix_load.wait()
        if 2 <= point <= 5:
            local_rows((point - 2) * (row_count // 4))

    def finish(row, spectral):
        activation, derivative = gelu_parts(spectral + conv[row])
        out_ref[row] = (fields_ref[row].astype(jnp.float32) + activation).astype(jnp.bfloat16)
        grad_mix[row] = (cotangent[row].astype(jnp.float32) * derivative).astype(jnp.bfloat16)

    def follow(number):
        begin_back(number)
        send_back(number)

    for number in range(CHUNKS):
        begin(number)
        if number == 0:
            wait_entry()
        send(number)
    cotangent_load.wait()
    run(fill, finish, follow)

    def adjoint_rows(first, count):
        def one(row):
            spare = jnp.zeros((lanes - kernel_count * width, channels), jnp.bfloat16)
            grads = lax.dot_general(
                whole[row].astype(jnp.bfloat16),
                weight_ref[...],
                (((1,), (1,)), ((), ())),
                preferred_element_type=jnp.float32,
            ).astype(jnp.bfloat16)
            stacked = jnp.concatenate(
                [grads[:, k * channels : (k + 1) * channels] for k in range(kernel_count)] + [spare],
                axis=0,
            )
            spread = jnp.dot(
                toeplitz(back_taps_ref[row], lon_dev), stacked, preferred_element_type=jnp.float32
            )
            for band in range(band_count):
                pieces[row, band] = spread[band * lon_dev : (band + 1) * lon_dev]

        def body(index, carry):
            for step in range(4):
                one(first + 4 * index + step)
            return carry

        lax.fori_loop(0, count // 4, body, 0)

    def gathered(row, full_first, full_last):
        total = cotangent[row].astype(jnp.float32)
        for band in range(band_count):
            offsets = range(2 * HW + 1)
            if band == 0 and not full_first:
                offsets = [2 * HW]
            if band == band_count - 1 and not full_last:
                offsets = [0]
            for offset in offsets:
                hit = near_ref[row + offset, band] == row
                total = total + jnp.where(hit, 1.0, 0.0) * pieces[row + offset, band]
        conv[row] = total

    quarter = tall // 4
    shares = (
        (0, quarter + 4),
        (quarter + 4, quarter - 4),
        (2 * quarter, quarter),
        (3 * quarter, quarter),
    )

    def fill_back(point):
        if point == 1:
            halos_back()
            stretch(grad_padded, whole)
        if 1 <= point <= 4:
            adjoint_rows(*shares[point - 1])
        if point == 5:
            gathered(0, True, False)
            gathered(row_count - 1, False, True)

            def body(row, carry):
                gathered(row, False, False)
                return carry

            lax.fori_loop(1, row_count - 1, body, 0)

    def finish_back(row, spectral):
        grad_ref[row] = (conv[row] + spectral).astype(jnp.bfloat16)

    run_back(fill_back, finish_back, lambda number: None)
    for copy in started:
        copy.wait_send()


def settle_kernel(first_in, second_in, first_out, second_out):
    first_out[...] = first_in[...]
    second_out[...] = second_in[...]


def pass_scratch(lat_count, lon_count, row_count, order_share, degree_dev, channels):
    share = lat_count * order_share
    wide = 2 * channels
    chips = lon_count // 2
    bf16 = jnp.bfloat16
    part = pltpu.VMEM((chips, row_count, 2 * share, channels), bf16)
    rows = pltpu.VMEM((lat_count, order_share, 2, row_count, channels), bf16)
    degrees = pltpu.VMEM((lat_count, order_share, degree_dev, wide), bf16)
    return [
        pltpu.VMEM((2, chips, row_count, 2 * share, channels), bf16),
        part,
        part,
        part,
        rows,
        rows,
        degrees,
        degrees,
        degrees,
        degrees,
        rows,
        rows,
        pltpu.VMEM((row_count, 2 * share, channels), bf16),
        pltpu.VMEM((lon_count, row_count, 2 * share, channels), bf16),
        pltpu.VMEM((degree_dev // CHUNKS, share, wide), jnp.float32),
        pltpu.SemaphoreType.DMA((2, CHUNKS)),
        pltpu.SemaphoreType.DMA((2, CHUNKS, chips)),
        pltpu.SemaphoreType.DMA((2, 4, CHUNKS, lat_count)),
        pltpu.SemaphoreType.DMA((2, CHUNKS, lon_count)),
        pltpu.SemaphoreType.DMA((2, CHUNKS, lon_count)),
        pltpu.SemaphoreType.DMA((2, 9)),
    ]


def tap_rows(basis, width):
    flat = jnp.pad(basis, ((0, 0), (0, 0), (0, 0), (0, width - basis.shape[3])))
    flat = flat.reshape(basis.shape[0], basis.shape[1], basis.shape[2] * width)
    lanes = -(-flat.shape[2] // 128) * 128
    return jnp.pad(flat, ((0, 0), (0, 0), (0, lanes - flat.shape[2]))).astype(jnp.float32)


def per_device(fields, cotangent, spectral_weight, local_weight, filter_basis, neighbor_rows):
    lat_count = lax.axis_size("lat")
    lon_count = lax.axis_size("lon")
    lat_index = lax.axis_index("lat")
    lon_index = lax.axis_index("lon")
    _, lat_dev, lon_dev, channels = fields.shape
    degree_dev = spectral_weight.shape[0]
    total_lat = lat_dev * lat_count
    total_lon = lon_dev * lon_count
    order_share = MDEV // lat_count
    width = lon_dev + 2 * HW
    tall = lat_dev + 2 * HW
    to_modes, from_modes = mode_tables(total_lon, MDEV * lon_count)
    table_shape = (lon_dev, 2, lon_count, lat_count, order_share)
    to_modes = lax.dynamic_slice_in_dim(to_modes, lon_index * lon_dev, lon_dev, 0)
    from_modes = lax.dynamic_slice_in_dim(from_modes, lon_index * lon_dev, lon_dev, 0)
    to_modes = to_modes.reshape(table_shape).transpose(0, 2, 3, 4, 1).reshape(lon_dev, -1)
    from_modes = from_modes.reshape(table_shape).transpose(0, 2, 3, 4, 1).reshape(lon_dev, -1)
    orders = (
        lon_index * MDEV + lat_index * order_share + jnp.arange(order_share, dtype=jnp.int32)
    )
    gain, back_gain, trig = legendre_inputs(orders, degree_dev * lat_count, total_lat)
    row_base = lat_index * lat_dev
    near_rows = lax.dynamic_slice_in_dim(
        jnp.pad(neighbor_rows, ((HW, HW), (0, 0))), row_base, tall, 0
    )
    near_basis = lax.dynamic_slice_in_dim(
        jnp.pad(filter_basis, ((0, 0), (HW, HW), (0, 0), (0, 0))), row_base, tall, 1
    )
    taps = tap_rows(near_basis[:, HW : HW + lat_dev].transpose(1, 0, 2, 3), width)
    back_taps = tap_rows(near_basis[..., ::-1].transpose(1, 2, 0, 3), width)
    smem = pl.BlockSpec(memory_space=pltpu.SMEM)
    vmem = pl.BlockSpec(memory_space=pltpu.VMEM)
    grid = jax.ShapeDtypeStruct((lat_dev, lon_dev, channels), jnp.bfloat16)
    bf16 = jnp.bfloat16
    table = pltpu.VMEM((order_share, degree_dev * lat_count, total_lat), bf16)
    rim = pltpu.VMEM((tall, lon_dev + 2 * EDGE, channels), bf16)
    passes = pass_scratch(lat_count, lon_count, lat_dev, order_share, degree_dev, channels)
    block_output, input_grad = pl.pallas_call(
        functools.partial(whole_kernel, lat_count, lon_count),
        out_shape=(grid, grid),
        in_specs=[smem] * 4 + [vmem] * 7 + [pl.BlockSpec(memory_space=pl.ANY)] * 2,
        out_specs=(vmem, vmem),
        scratch_shapes=[
            table,
            table,
            pltpu.VMEM(spectral_weight.shape, bf16),
            pltpu.VMEM((lat_dev, lon_dev, channels), bf16),
            rim,
            rim,
            pltpu.VMEM((tall, width, channels), jnp.float32),
            pltpu.VMEM((lat_dev, lon_dev, channels), jnp.float32),
            pltpu.VMEM((lat_dev, lon_dev, channels), bf16),
            pltpu.VMEM((tall, filter_basis.shape[2], lon_dev, channels), jnp.float32),
            pltpu.VMEM(to_modes.shape, bf16),
            pltpu.VMEM(to_modes.shape, bf16),
            pltpu.SemaphoreType.DMA((2,)),
        ]
        + passes
        + passes,
        compiler_params=pltpu.CompilerParams(
            collective_id=0, has_side_effects=True, vmem_limit_bytes=56 * 1024 * 1024
        ),
        name="operator_block",
    )(
        gain,
        back_gain,
        orders,
        near_rows - row_base,
        trig,
        fields[0],
        to_modes.T,
        from_modes.T,
        taps,
        back_taps,
        local_weight.reshape(-1, channels),
        cotangent[0],
        spectral_weight,
    )
    quarter = pl.BlockSpec((lat_dev // 4, lon_dev, channels), lambda index: (index, 0, 0))
    block_output, input_grad = pl.pallas_call(
        settle_kernel,
        grid=(4,),
        out_shape=(grid, grid),
        in_specs=[quarter] * 2,
        out_specs=(quarter, quarter),
        compiler_params=pltpu.CompilerParams(vmem_limit_bytes=56 * 1024 * 1024),
        name="settle",
    )(block_output, input_grad)
    return (block_output[None], input_grad[None])


def solution(mesh):
    in_specs = (
        P(None, "lat", "lon", None),
        P(None, "lat", "lon", None),
        P("lat", None, None, None),
        P(),
        P(),
        P(),
    )
    out_specs = (P(None, "lat", "lon", None), P(None, "lat", "lon", None))
    return jax.shard_map(
        per_device, mesh=mesh, in_specs=in_specs, out_specs=out_specs, check_vma=False
    )
```

```python
import functools
import math

import jax
import jax.numpy as jnp
from jax import lax
from jax.experimental import pallas as pl
from jax.experimental.pallas import tpu as pltpu
from jax.sharding import PartitionSpec as P

MDEV = 16
HW = 8


TANH_SCALE = 0.7978845608028654
CUBIC_TERM = 0.044715


def gelu_parts(values):
    tanh_input = TANH_SCALE * (values + CUBIC_TERM * values * values * values)
    hyper = jnp.tanh(tanh_input)
    result = 0.5 * values * (1.0 + hyper)
    derivative = 0.5 * (1.0 + hyper) + 0.5 * values * (1.0 - hyper * hyper) * TANH_SCALE * (
        1.0 + 3.0 * CUBIC_TERM * values * values
    )
    return (result, derivative)


def mode_tables(lon_count, mode_count):
    angles_int = (
        jnp.arange(lon_count, dtype=jnp.int32)[:, None]
        * jnp.arange(mode_count, dtype=jnp.int32)[None, :]
        % lon_count
    )
    angles = angles_int.astype(jnp.float32) * (2.0 * math.pi / lon_count)
    stacked = jnp.stack([jnp.cos(angles), -jnp.sin(angles)], axis=1)
    orders = jnp.arange(mode_count, dtype=jnp.int32)
    factor = jnp.where(orders == 0, 1.0, 2.0).astype(jnp.float32)
    to_modes = (stacked * (2.0 * math.pi / lon_count)).astype(jnp.bfloat16)
    from_modes = (stacked * factor[None, None, :]).astype(jnp.bfloat16)
    return (to_modes, from_modes)


STEP = 16


def legendre_kernel(gain_ref, back_ref, orders_ref, trig_ref, weighted_ref, plain_ref):
    order_share, degree_count, _ = plain_ref.shape
    cosine = trig_ref[0:1, :]
    quadrature = trig_ref[1:2, :]

    def block(index, state):
        carried = []
        for e in range(order_share):
            value, previous, log_scale = state[3 * e : 3 * e + 3]
            order = orders_ref[e]
            rows = []
            for step in range(STEP):
                degree = index * STEP + step
                active = degree > order
                following = gain_ref[e, degree] * (cosine * value) - back_ref[e, degree] * previous
                previous = jnp.where(active, value, previous)
                value = jnp.where(active, following, value)
                rows.append(jnp.where(degree >= order, value, 0.0))
            stacked = jnp.concatenate(rows, axis=0) * jnp.exp(log_scale)
            place = pl.ds(pl.multiple_of(index * STEP, STEP), STEP)
            plain_ref[e, place, :] = stacked.astype(jnp.bfloat16)
            weighted_ref[e, place, :] = (stacked * quadrature).astype(jnp.bfloat16)
            largest = jnp.maximum(jnp.abs(value), jnp.abs(previous))
            carried += [value / largest, previous / largest, log_scale + jnp.log(largest)]
        return tuple(carried)

    start = []
    for e in range(order_share):
        seed = trig_ref[2 + e : 3 + e, :]
        start += [jnp.ones_like(seed), jnp.zeros_like(seed), seed]
    lax.fori_loop(0, degree_count // STEP, block, tuple(start))


def legendre_inputs(orders, degree_count, lat_count):
    order_share = orders.shape[0]
    colatitude = math.pi * (jnp.arange(lat_count, dtype=jnp.float32) + 0.5) / lat_count
    sine_part = jnp.sin(colatitude)
    order_real = orders.astype(jnp.float32)
    seed_log = 0.5 * (
        jnp.log((2.0 * order_real + 1.0) / (4.0 * math.pi))
        + lax.lgamma(order_real + 0.5)
        - lax.lgamma(order_real + 1.0)
        - 0.5 * math.log(math.pi)
    )
    seed_log = seed_log[:, None] + order_real[:, None] * jnp.log(sine_part)[None, :]
    degree_real = jnp.arange(degree_count, dtype=jnp.float32)[None, :]
    order_row = order_real[:, None]
    forward_gain = jnp.sqrt(
        jnp.maximum(4.0 * degree_real * degree_real - 1.0, 1.0)
        / jnp.maximum(degree_real * degree_real - order_row * order_row, 1.0)
    )
    backward_gain = jnp.sqrt(
        jnp.maximum((degree_real - 1.0) ** 2 - order_row * order_row, 0.0)
        / jnp.maximum(4.0 * (degree_real - 1.0) ** 2 - 1.0, 1.0)
    )
    trig = jnp.concatenate(
        [
            jnp.cos(colatitude)[None, :],
            (math.pi / lat_count * sine_part)[None, :],
            seed_log,
        ],
        axis=0,
    )
    return (forward_gain, forward_gain * backward_gain, trig)


CHUNKS = 2
SUPPORT = 2 * HW + 1
EDGE = 2 * HW


def place_of(lat_count, lon_count):
    lat_me = lax.axis_index("lat")
    lon_me = lax.axis_index("lon")
    return lat_me, lon_me


def enter(lat_count, lon_count):
    lat_me, lon_me = place_of(lat_count, lon_count)
    barrier = pltpu.get_barrier_semaphore()

    def greet(lat, lon):
        pl.semaphore_signal(
            barrier, inc=1, device_id=(lat, lon), device_id_type=pl.DeviceIdType.MESH
        )

    for step in range(1, lat_count):
        greet(lax.rem(lat_me + step, lat_count), lon_me)
    for step in range(1, lon_count):
        greet(lat_me, lax.rem(lon_me + step, lon_count))
    for lat_step in (1, lat_count - 1):
        for lon_step in (1, lon_count - 1):
            greet(lax.rem(lat_me + lat_step, lat_count), lax.rem(lon_me + lon_step, lon_count))
    return lambda: pl.semaphore_wait(barrier, lat_count - 1 + lon_count - 1 + 4)


def spectral_pass(
    lat_count,
    lon_count,
    adjoint,
    started,
    data_ref,
    first_ref,
    down_ref,
    up_ref,
    last_ref,
    mix_ref,
    padded_ref,
    part_out,
    pair_in,
    pair_out,
    cross_in,
    rows_out,
    rows_in,
    deg_out,
    deg_in,
    mixed_out,
    mixed_in,
    zonal_out,
    zonal_in,
    grid_out,
    grid_in,
    blended,
    pair_sems,
    cross_sems,
    lat_sems,
    gather_sems,
    relay_sems,
    halo_sems,
):
    row_count, lon_dev, channels = data_ref.shape
    order_share = down_ref.shape[0]
    degree_dev = mix_ref.shape[0]
    wide = 2 * channels
    share = lat_count * order_share
    modes = 2 * share
    chips = lon_count // 2
    rows_each = row_count // CHUNKS
    degrees_each = degree_dev // CHUNKS
    lat_me = lax.axis_index("lat")
    lon_me = lax.axis_index("lon")
    chip = lon_me // 2
    core = lax.rem(lon_me, 2)
    mate = 2 * chip + 1 - core
    lat_peers = [lax.rem(lat_me + step, lat_count) for step in range(1, lat_count)]
    chip_peers = [lax.rem(chip + step, chips) for step in range(1, chips)]
    lat_next = lax.rem(lat_me + 1, lat_count)
    lat_last = lax.rem(lat_me + lat_count - 1, lat_count)
    lon_next = lax.rem(lon_me + 1, lon_count)
    lon_last = lax.rem(lon_me + lon_count - 1, lon_count)
    halo_rows = {
        0: (lat_me, slice(0, row_count), slice(HW, HW + row_count)),
        1: (lat_next, slice(row_count - HW, row_count), slice(0, HW)),
        2: (lat_last, slice(0, HW), slice(HW + row_count, 2 * HW + row_count)),
    }
    halo_columns = {
        0: (lon_me, slice(0, lon_dev), slice(EDGE, EDGE + lon_dev)),
        1: (lon_next, slice(lon_dev - EDGE, lon_dev), slice(0, EDGE)),
        2: (lon_last, slice(0, EDGE), slice(EDGE + lon_dev, 2 * EDGE + lon_dev)),
    }

    def copying(source, target, sems, place, came, device):
        return pltpu.make_async_remote_copy(
            src_ref=source,
            dst_ref=target,
            send_sem=sems.at[(0,) + place],
            recv_sem=sems.at[(1,) + came],
            device_id=device,
            device_id_type=pl.DeviceIdType.MESH,
        )

    def push(source, target, sems, place, came, device):
        copy = copying(source, target, sems, place, came, device)
        copy.start()
        started.append(copy)

    def arrived(target, sems, came):
        copying(target, target, sems, came, came, (lat_me, mate)).wait_recv()

    def rows_of(number):
        return pl.ds(number * rows_each, rows_each)

    def transform(number):
        group = 8

        def body(index, carry):
            for step in range(group):
                row = number * rows_each + index * group + step
                part = jnp.dot(
                    first_ref[...], data_ref[row], preferred_element_type=jnp.float32
                ).astype(jnp.bfloat16)
                for other in range(chips):
                    for side in range(2):
                        begin = (2 * other + side) * modes
                        part_out[side, other, row] = part[begin : begin + modes]
            return carry

        lax.fori_loop(0, rows_each // group, body, 0)

    def lat_push(number, piece, source, target):
        for peer in lat_peers:
            push(
                source(peer),
                target(lat_me),
                lat_sems,
                (number, piece, peer),
                (number, piece, lat_me),
                (peer, lon_me),
            )

    def lat_arrived(number, piece, target):
        for peer in lat_peers:
            arrived(target(peer), lat_sems, (number, piece, peer))

    def begin(number):
        transform(number)

    def send(number):
        push(
            part_out.at[1 - core, :, rows_of(number)],
            pair_in.at[:, rows_of(number)],
            pair_sems,
            (number,),
            (number,),
            (lat_me, mate),
        )

    def halos_arrived():
        for r, (_, _, to_rows) in halo_rows.items():
            for c, (_, _, to_columns) in halo_columns.items():
                if r or c:
                    arrived(padded_ref.at[to_rows, to_columns], halo_sems, (3 * r + c,))

    def run(fill, finish, follow):
        for r, (lat, from_rows, to_rows) in halo_rows.items():
            for c, (lon, from_columns, to_columns) in halo_columns.items():
                if r or c:
                    push(
                        data_ref.at[from_rows, from_columns],
                        padded_ref.at[to_rows, to_columns],
                        halo_sems,
                        (3 * r + c,),
                        (3 * r + c,),
                        (lat, lon),
                    )
        for number in range(CHUNKS):
            piece = rows_of(number)
            arrived(pair_in.at[:, piece], pair_sems, (number,))
            for other in chip_peers:
                pair_out[other, piece] = (
                    part_out[core, other, piece].astype(jnp.float32)
                    + pair_in[other, piece].astype(jnp.float32)
                ).astype(jnp.bfloat16)
                push(
                    pair_out.at[other, piece],
                    cross_in.at[chip, piece],
                    cross_sems,
                    (number, other),
                    (number, chip),
                    (lat_me, 2 * other + core),
                )
        padded_ref[HW : HW + row_count, EDGE : EDGE + lon_dev] = data_ref[...]
        fill(0)
        for number in range(CHUNKS):
            piece = rows_of(number)
            total = part_out[core, chip, piece].astype(jnp.float32) + pair_in[chip, piece].astype(
                jnp.float32
            )
            for other in chip_peers:
                arrived(cross_in.at[other, piece], cross_sems, (number, other))
                total = total + cross_in[other, piece].astype(jnp.float32)
            begin = number * rows_each
            rows_out[:, :, :, begin : begin + rows_each] = (
                jnp.swapaxes(total, 0, 1)
                .astype(jnp.bfloat16)
                .reshape(lat_count, order_share, 2, rows_each, channels)
            )
            lat_push(
                0,
                number,
                lambda peer: rows_out.at[peer, :, :, piece],
                lambda peer: rows_in.at[peer, :, :, piece],
            )
        rows_in[lat_me] = rows_out[lat_me]
        fill(1)
        for number in range(CHUNKS):
            piece = rows_of(number)
            lat_arrived(0, number, lambda peer: rows_in.at[peer, :, :, piece])

        for e in range(order_share):
            columns = jnp.concatenate(
                [rows_in[:, e, part].reshape(lat_count * row_count, channels) for part in range(2)],
                axis=1,
            )
            degrees = jnp.dot(down_ref[e], columns, preferred_element_type=jnp.float32)
            deg_out[:, e] = degrees.astype(jnp.bfloat16).reshape(lat_count, degree_dev, wide)
        for number in range(CHUNKS):
            piece = pl.ds(number * degrees_each, degrees_each)
            lat_push(
                1,
                number,
                lambda peer: deg_out.at[peer, :, piece],
                lambda peer: deg_in.at[peer, :, piece],
            )
        deg_in[lat_me] = deg_out[lat_me]
        fill(2)

        for number in range(CHUNKS):
            begin = number * degrees_each
            piece = pl.ds(begin, degrees_each)
            lat_arrived(1, number, lambda peer: deg_in.at[peer, :, piece])
            by_degree = deg_in[:, :, begin : begin + degrees_each].reshape(share, degrees_each, wide)
            turned = jnp.swapaxes(by_degree.astype(jnp.float32), 0, 1).astype(jnp.bfloat16)
            for step in range(degrees_each):
                degree = begin + step
                pair = jnp.concatenate([turned[step, :, :channels], turned[step, :, channels:]], axis=0)
                if adjoint:
                    weights = jnp.concatenate([mix_ref[degree, 0], mix_ref[degree, 1]], axis=0)
                    product = lax.dot_general(
                        pair, weights, (((1,), (1,)), ((), ())), preferred_element_type=jnp.float32
                    )
                else:
                    weights = jnp.concatenate([mix_ref[degree, 0], mix_ref[degree, 1]], axis=1)
                    product = jnp.dot(pair, weights, preferred_element_type=jnp.float32)
                sign = -1.0 if adjoint else 1.0
                blended[step, :, :channels] = (
                    product[:share, :channels] - sign * product[share:, channels:]
                )
                blended[step, :, channels:] = (
                    sign * product[:share, channels:] + product[share:, :channels]
                )
            mixed_out[:, :, begin : begin + degrees_each] = (
                jnp.swapaxes(blended[...], 0, 1)
                .astype(jnp.bfloat16)
                .reshape(lat_count, order_share, degrees_each, wide)
            )
            lat_push(
                2,
                number,
                lambda peer: mixed_out.at[peer, :, piece],
                lambda peer: mixed_in.at[peer, :, piece],
            )
        mixed_in[lat_me] = mixed_out[lat_me]
        fill(3)
        for number in range(CHUNKS):
            piece = pl.ds(number * degrees_each, degrees_each)
            lat_arrived(2, number, lambda peer: mixed_in.at[peer, :, piece])

        for e in range(order_share):
            spectrum = mixed_in[:, e].reshape(lat_count * degree_dev, wide)
            zonal = lax.dot_general(
                up_ref[e], spectrum, (((0,), (0,)), ((), ())), preferred_element_type=jnp.float32
            ).astype(jnp.bfloat16)
            for part in range(2):
                zonal_out[:, e, part] = zonal[:, part * channels : (part + 1) * channels].reshape(
                    lat_count, row_count, channels
                )
        for number in range(CHUNKS):
            piece = rows_of(number)
            lat_push(
                3,
                number,
                lambda peer: zonal_out.at[peer, :, :, piece],
                lambda peer: zonal_in.at[peer, :, :, piece],
            )
        zonal_in[lat_me] = zonal_out[lat_me]
        fill(4)

        for number in range(CHUNKS):
            piece = rows_of(number)
            begin = number * rows_each
            lat_arrived(3, number, lambda peer: zonal_in.at[peer, :, :, piece])
            by_order = zonal_in[:, :, :, begin : begin + rows_each].reshape(modes, rows_each, channels)
            grid_out[piece] = jnp.swapaxes(by_order.astype(jnp.float32), 0, 1).astype(jnp.bfloat16)
            for lon in [2 * other + core for other in chip_peers] + [mate]:
                push(
                    grid_out.at[piece],
                    grid_in.at[lon_me, piece],
                    gather_sems,
                    (number, lon),
                    (number, lon_me),
                    (lat_me, lon),
                )
            grid_in[lon_me, piece] = grid_out[piece]
        fill(5)
        for number in range(CHUNKS):
            piece = rows_of(number)
            for other in chip_peers:
                slot = 2 * other + core
                arrived(grid_in.at[slot, piece], gather_sems, (number, slot))
                push(
                    grid_in.at[slot, piece],
                    grid_in.at[slot, piece],
                    relay_sems,
                    (number, slot),
                    (number, slot),
                    (lat_me, mate),
                )
        for number in range(CHUNKS):
            piece = rows_of(number)
            arrived(grid_in.at[mate, piece], gather_sems, (number, mate))
            for other in chip_peers:
                slot = 2 * other + 1 - core
                arrived(grid_in.at[slot, piece], relay_sems, (number, slot))

            def restore(index, carry):
                for step in range(8):
                    row = number * rows_each + index * 8 + step
                    every = grid_in[:, row].reshape(lon_count * modes, channels)
                    finish(
                        row,
                        jnp.dot(last_ref[...], every, preferred_element_type=jnp.float32)
                        .astype(jnp.bfloat16)
                        .astype(jnp.float32),
                    )
                return carry

            lax.fori_loop(0, rows_each // 8, restore, 0)
            follow(number)


    return begin, send, run, halos_arrived


def toeplitz(taps, count):
    spread = [
        pltpu.roll(
            jnp.broadcast_to(taps[k : k + 1, :], (count, taps.shape[1])),
            0,
            1,
            stride=1,
            stride_axis=0,
        )
        for k in range(taps.shape[0])
    ]
    return jnp.concatenate(spread, axis=0).astype(jnp.bfloat16)


def stretch(padded_ref, whole_ref):
    width = whole_ref.shape[1]

    def body(row, carry):
        whole_ref[row] = padded_ref[row].astype(jnp.float32)[HW : HW + width]
        return carry

    lax.fori_loop(0, whole_ref.shape[0], body, 0)


def whole_kernel(
    lat_count,
    lon_count,
    gain_ref,
    back_ref,
    orders_ref,
    near_ref,
    trig_ref,
    fields_ref,
    to_rows_ref,
    from_rows_ref,
    taps_ref,
    weight_ref,
    cotangent_any,
    mix_any,
    out_ref,
    grad_ref,
    weighted,
    plain,
    mix,
    cotangent,
    padded,
    grad_padded,
    whole,
    conv,
    grad_mix,
    pieces,
    to_ref,
    from_ref,
    load_sems,
    *scratch,
):
    row_count, lon_dev, channels = fields_ref.shape
    tall, width, _ = whole.shape
    kernel_count = weight_ref.shape[0] // channels
    band_count = near_ref.shape[1]
    lanes = -(-max(kernel_count, band_count) * width // 128) * 128
    wait_entry = enter(lat_count, lon_count)
    mix_load = pltpu.make_async_copy(mix_any, mix, load_sems.at[0])
    cotangent_load = pltpu.make_async_copy(cotangent_any, cotangent, load_sems.at[1])
    mix_load.start()
    cotangent_load.start()
    started = []
    half = len(scratch) // 2
    begin, send, run, halos = spectral_pass(
        lat_count,
        lon_count,
        False,
        started,
        fields_ref,
        to_rows_ref,
        weighted,
        plain,
        from_ref,
        mix,
        padded,
        *scratch[:half],
    )
    begin_back, send_back, run_back, halos_back = spectral_pass(
        lat_count,
        lon_count,
        True,
        started,
        grad_mix,
        from_rows_ref,
        plain,
        weighted,
        to_ref,
        mix,
        grad_padded,
        *scratch[half:],
    )

    def tap_lines(row, shift, line_count, block_count, line_stride, block_stride):
        taps = taps_ref[row]
        if shift:
            taps = pltpu.roll(taps, taps.shape[1] - shift, 1)
        lane = lax.broadcasted_iota(jnp.int32, taps.shape, 1)
        taps = jnp.where(lane < SUPPORT, taps, 0.0)
        taps = jnp.concatenate(
            [taps, jnp.zeros((taps.shape[0], lanes - taps.shape[1]), jnp.float32)], axis=1
        )
        moved = [taps] + [pltpu.roll(taps, block * width, 1) for block in range(1, block_count)]
        lines = []
        for line in range(line_count):
            total = 0.0
            for block in range(block_count):
                index = line * line_stride + block * block_stride
                total = total + moved[block][index : index + 1]
            lines.append(total)
        return jnp.concatenate(lines, axis=0)

    def local_rows(first):
        def one(row):
            spare = jnp.zeros((lanes - band_count * width, channels), jnp.float32)
            sources = jnp.concatenate(
                [whole[near_ref[row + HW, band] + HW] for band in range(band_count)] + [spare], axis=0
            ).astype(jnp.bfloat16)
            terms = jnp.dot(
                toeplitz(tap_lines(row + HW, 0, kernel_count, band_count, band_count, 1), lon_dev), sources, preferred_element_type=jnp.float32
            ).astype(jnp.bfloat16)
            flat = jnp.concatenate(
                [terms[k * lon_dev : (k + 1) * lon_dev] for k in range(kernel_count)], axis=1
            )
            conv[row] = jnp.dot(flat, weight_ref[...], preferred_element_type=jnp.float32)

        def body(index, carry):
            for step in range(4):
                one(first + 4 * index + step)
            return carry

        lax.fori_loop(0, row_count // 16, body, 0)

    def fill(point):
        if point == 0:
            for rows_ref, columns_ref in ((to_rows_ref, to_ref), (from_rows_ref, from_ref)):
                columns_ref[...] = rows_ref[...].astype(jnp.float32).T.astype(jnp.bfloat16)
        if point == 1:
            legendre_kernel(gain_ref, back_ref, orders_ref, trig_ref, weighted, plain)
            halos()
            stretch(padded, whole)
        if point == 2:
            mix_load.wait()
        if 2 <= point <= 5:
            local_rows((point - 2) * (row_count // 4))

    def finish(row, spectral):
        activation, derivative = gelu_parts(spectral + conv[row])
        out_ref[row] = (fields_ref[row].astype(jnp.float32) + activation).astype(jnp.bfloat16)
        grad_mix[row] = (cotangent[row].astype(jnp.float32) * derivative).astype(jnp.bfloat16)

    def follow(number):
        begin_back(number)
        send_back(number)

    for number in range(CHUNKS):
        begin(number)
        if number == 0:
            wait_entry()
        send(number)
    cotangent_load.wait()
    run(fill, finish, follow)

    def adjoint_rows(first, count):
        def one(row):
            spare = jnp.zeros((lanes - kernel_count * width, channels), jnp.bfloat16)
            grads = lax.dot_general(
                whole[row].astype(jnp.bfloat16),
                weight_ref[...],
                (((1,), (1,)), ((), ())),
                preferred_element_type=jnp.float32,
            ).astype(jnp.bfloat16)
            stacked = jnp.concatenate(
                [grads[:, k * channels : (k + 1) * channels] for k in range(kernel_count)] + [spare],
                axis=0,
            )
            spread = jnp.dot(
                toeplitz(tap_lines(row, SUPPORT, band_count, kernel_count, 1, band_count), lon_dev), stacked, preferred_element_type=jnp.float32
            )
            for band in range(band_count):
                pieces[row, band] = spread[band * lon_dev : (band + 1) * lon_dev]

        def body(index, carry):
            for step in range(4):
                one(first + 4 * index + step)
            return carry

        lax.fori_loop(0, count // 4, body, 0)

    def gathered(row, full_first, full_last):
        total = cotangent[row].astype(jnp.float32)
        for band in range(band_count):
            offsets = range(2 * HW + 1)
            if band == 0 and not full_first:
                offsets = [2 * HW]
            if band == band_count - 1 and not full_last:
                offsets = [0]
            for offset in offsets:
                hit = near_ref[row + offset, band] == row
                total = total + jnp.where(hit, 1.0, 0.0) * pieces[row + offset, band]
        conv[row] = total

    quarter = tall // 4
    shares = (
        (0, quarter + 4),
        (quarter + 4, quarter - 4),
        (2 * quarter, quarter),
        (3 * quarter, quarter),
    )

    def fill_back(point):
        if point == 1:
            halos_back()
            stretch(grad_padded, whole)
        if 1 <= point <= 4:
            adjoint_rows(*shares[point - 1])
        if point == 5:
            gathered(0, True, False)
            gathered(row_count - 1, False, True)

            def body(row, carry):
                gathered(row, False, False)
                return carry

            lax.fori_loop(1, row_count - 1, body, 0)

    def finish_back(row, spectral):
        grad_ref[row] = (conv[row] + spectral).astype(jnp.bfloat16)

    run_back(fill_back, finish_back, lambda number: None)
    for copy in started:
        copy.wait_send()


def settle_kernel(first_in, second_in, first_out, second_out):
    first_out[...] = first_in[...]
    second_out[...] = second_in[...]


def pass_scratch(lat_count, lon_count, row_count, order_share, degree_dev, channels):
    share = lat_count * order_share
    wide = 2 * channels
    chips = lon_count // 2
    bf16 = jnp.bfloat16
    part = pltpu.VMEM((chips, row_count, 2 * share, channels), bf16)
    rows = pltpu.VMEM((lat_count, order_share, 2, row_count, channels), bf16)
    degrees = pltpu.VMEM((lat_count, order_share, degree_dev, wide), bf16)
    return [
        pltpu.VMEM((2, chips, row_count, 2 * share, channels), bf16),
        part,
        part,
        part,
        rows,
        rows,
        degrees,
        degrees,
        degrees,
        degrees,
        rows,
        rows,
        pltpu.VMEM((row_count, 2 * share, channels), bf16),
        pltpu.VMEM((lon_count, row_count, 2 * share, channels), bf16),
        pltpu.VMEM((degree_dev // CHUNKS, share, wide), jnp.float32),
        pltpu.SemaphoreType.DMA((2, CHUNKS)),
        pltpu.SemaphoreType.DMA((2, CHUNKS, chips)),
        pltpu.SemaphoreType.DMA((2, 4, CHUNKS, lat_count)),
        pltpu.SemaphoreType.DMA((2, CHUNKS, lon_count)),
        pltpu.SemaphoreType.DMA((2, CHUNKS, lon_count)),
        pltpu.SemaphoreType.DMA((2, 9)),
    ]


def tap_rows(basis):
    both = jnp.concatenate([basis, basis[..., ::-1]], axis=3).transpose(1, 0, 2, 3)
    flat = both.reshape(both.shape[0], both.shape[1] * both.shape[2], both.shape[3])
    rows = -(-flat.shape[1] // 8) * 8
    return jnp.pad(
        flat, ((0, 0), (0, rows - flat.shape[1]), (0, 128 - flat.shape[2]))
    ).astype(jnp.float32)


def per_device(fields, cotangent, spectral_weight, local_weight, filter_basis, neighbor_rows):
    lat_count = lax.axis_size("lat")
    lon_count = lax.axis_size("lon")
    lat_index = lax.axis_index("lat")
    lon_index = lax.axis_index("lon")
    _, lat_dev, lon_dev, channels = fields.shape
    degree_dev = spectral_weight.shape[0]
    total_lat = lat_dev * lat_count
    total_lon = lon_dev * lon_count
    order_share = MDEV // lat_count
    width = lon_dev + 2 * HW
    tall = lat_dev + 2 * HW
    to_modes, from_modes = mode_tables(total_lon, MDEV * lon_count)
    table_shape = (lon_dev, 2, lon_count, lat_count, order_share)
    to_modes = lax.dynamic_slice_in_dim(to_modes, lon_index * lon_dev, lon_dev, 0)
    from_modes = lax.dynamic_slice_in_dim(from_modes, lon_index * lon_dev, lon_dev, 0)
    to_modes = to_modes.reshape(table_shape).transpose(0, 2, 3, 4, 1).reshape(lon_dev, -1)
    from_modes = from_modes.reshape(table_shape).transpose(0, 2, 3, 4, 1).reshape(lon_dev, -1)
    orders = (
        lon_index * MDEV + lat_index * order_share + jnp.arange(order_share, dtype=jnp.int32)
    )
    gain, back_gain, trig = legendre_inputs(orders, degree_dev * lat_count, total_lat)
    row_base = lat_index * lat_dev
    near_rows = lax.dynamic_slice_in_dim(
        jnp.pad(neighbor_rows, ((HW, HW), (0, 0))), row_base, tall, 0
    )
    near_basis = lax.dynamic_slice_in_dim(
        jnp.pad(filter_basis, ((0, 0), (HW, HW), (0, 0), (0, 0))), row_base, tall, 1
    )
    taps = tap_rows(near_basis)
    smem = pl.BlockSpec(memory_space=pltpu.SMEM)
    vmem = pl.BlockSpec(memory_space=pltpu.VMEM)
    grid = jax.ShapeDtypeStruct((lat_dev, lon_dev, channels), jnp.bfloat16)
    bf16 = jnp.bfloat16
    table = pltpu.VMEM((order_share, degree_dev * lat_count, total_lat), bf16)
    rim = pltpu.VMEM((tall, lon_dev + 2 * EDGE, channels), bf16)
    passes = pass_scratch(lat_count, lon_count, lat_dev, order_share, degree_dev, channels)
    block_output, input_grad = pl.pallas_call(
        functools.partial(whole_kernel, lat_count, lon_count),
        out_shape=(grid, grid),
        in_specs=[smem] * 4 + [vmem] * 6 + [pl.BlockSpec(memory_space=pl.ANY)] * 2,
        out_specs=(vmem, vmem),
        scratch_shapes=[
            table,
            table,
            pltpu.VMEM(spectral_weight.shape, bf16),
            pltpu.VMEM((lat_dev, lon_dev, channels), bf16),
            rim,
            rim,
            pltpu.VMEM((tall, width, channels), jnp.float32),
            pltpu.VMEM((lat_dev, lon_dev, channels), jnp.float32),
            pltpu.VMEM((lat_dev, lon_dev, channels), bf16),
            pltpu.VMEM((tall, filter_basis.shape[2], lon_dev, channels), jnp.float32),
            pltpu.VMEM(to_modes.shape, bf16),
            pltpu.VMEM(to_modes.shape, bf16),
            pltpu.SemaphoreType.DMA((2,)),
        ]
        + passes
        + passes,
        compiler_params=pltpu.CompilerParams(
            collective_id=0, has_side_effects=True, vmem_limit_bytes=56 * 1024 * 1024
        ),
        name="operator_block",
    )(
        gain,
        back_gain,
        orders,
        near_rows - row_base,
        trig,
        fields[0],
        to_modes.T,
        from_modes.T,
        taps,
        local_weight.reshape(-1, channels),
        cotangent[0],
        spectral_weight,
    )
    quarter = pl.BlockSpec((lat_dev // 4, lon_dev, channels), lambda index: (index, 0, 0))
    block_output, input_grad = pl.pallas_call(
        settle_kernel,
        grid=(4,),
        out_shape=(grid, grid),
        in_specs=[quarter] * 2,
        out_specs=(quarter, quarter),
        compiler_params=pltpu.CompilerParams(vmem_limit_bytes=56 * 1024 * 1024),
        name="settle",
    )(block_output, input_grad)
    return (block_output[None], input_grad[None])


def solution(mesh):
    in_specs = (
        P(None, "lat", "lon", None),
        P(None, "lat", "lon", None),
        P("lat", None, None, None),
        P(),
        P(),
        P(),
    )
    out_specs = (P(None, "lat", "lon", None), P(None, "lat", "lon", None))
    return jax.shard_map(
        per_device, mesh=mesh, in_specs=in_specs, out_specs=out_specs, check_vma=False
    )
```
